32 devices in a mesh: fsdp: 4 (over y, x), context: 4 (over z), tensor: 2 (over core).
Axes of the slice: x: 2, y: 2, z: 4, core: 2. Of those that a mesh axis runs over, the one named last changes fastest.
Arguments:
- tokens: bfloat16 [4096, 1024], P(('fsdp', 'context')), may hold values from -6 to 6
- cotangent: bfloat16 [4096, 1024], P(('fsdp', 'context')), may hold values from -6 to 6
- ln1_gain: float32 [1024], replicated, may hold values from 0.25 to 1.75
- ln1_bias: float32 [1024], replicated, may hold values from -1.75 to 1.75
- ln2_gain: float32 [1024], replicated, may hold values from 0.25 to 1.75
- ln2_bias: float32 [1024], replicated, may hold values from -1.75 to 1.75
- w_qkv: bfloat16 [1024, 3, 1024], P('fsdp', None, 'tensor'), may hold values from -0.1875 to 0.1875
- b_qkv: float32 [3, 1024], P(None, 'tensor'), may hold values from -1.75 to 1.75
- w_out: bfloat16 [1024, 1024], P('fsdp', 'tensor'), may hold values from -3 to 3
- b_out: float32 [1024], replicated, may hold values from -1.75 to 1.75
- w_up: bfloat16 [1024, 4096], P('fsdp', 'tensor'), may hold values from -0.1875 to 0.1875
- b_up: float32 [4096], P('tensor'), may hold values from -1.75 to 1.75
- w_down: bfloat16 [1024, 4096], P('fsdp', 'tensor'), may hold values from -0.09375 to 0.09375
- b_down: float32 [1024], replicated, may hold values from -1.75 to 1.75
Outputs:
- output: bfloat16 [4096, 1024], P(('fsdp', 'context'))
- d_tokens: float32 [4096, 1024], P(('fsdp', 'context'))
- d_ln1_gain: float32 [1024], P(('fsdp', 'context'))
- d_ln1_bias: float32 [1024], P(('fsdp', 'context'))
- d_ln2_gain: float32 [1024], P(('fsdp', 'context'))
- d_ln2_bias: float32 [1024], P(('fsdp', 'context'))
- d_w_qkv: float32 [1024, 3, 1024], P(('fsdp', 'context'), None, 'tensor')
- d_b_qkv: float32 [3, 1024], P(None, 'tensor')
- d_w_out: float32 [1024, 1024], P(('fsdp', 'context'), 'tensor')
- d_b_out: float32 [1024], P(('fsdp', 'context'))
- d_w_up: float32 [1024, 4096], P(('fsdp', 'context'), 'tensor')
- d_b_up: float32 [4096], P('tensor')
- d_w_down: float32 [1024, 4096], P(('fsdp', 'context'), 'tensor')
- d_b_down: float32 [1024], P(('fsdp', 'context'))
The draws below stay inside these ranges and needn't reach their ends.
All inputs are finite; a program needn't handle non-finite values.
Results may differ from the reference program's by a relative error of at most 0.014.
Values may be sent and summed in bfloat16 or wider, within the bound.
No kernel may reach another device: no remote copies, remote signals or barrier semaphores. Data moves between devices by JAX's collectives and lax.ppermute only.
A program may use at most 128 MiB of HBM per device.

```python
import jax
import jax.numpy as jnp
from jax import lax

D = 1024
HEADS = 16
HEAD = 64
ROT = 16
FF = 4096
SEQ = 1024
SEQS = 4
TOKENS = 4096


def raised(array, rng, source, target, blocks, factor):
    def block_of(axis_at):
        return (jnp.arange(array.shape[axis_at]) // (array.shape[axis_at] // blocks)).reshape((-1,) + (1,) * (array.ndim - 1 - axis_at))

    near = jax.random.permutation(rng, blocks)[block_of(target)]
    other_side = (block_of(target) + blocks // 2) % blocks
    return jnp.where((block_of(source) == near) | (block_of(source) == other_side), factor * array, array)


def level_of(own_key, shape, cuts, least, largest):
    def one(axis_at, blocks):
        heights = jax.random.uniform(jax.random.fold_in(jax.random.fold_in(own_key, 6), axis_at), (blocks,), jnp.float32, least / len(cuts), largest / len(cuts))
        return jnp.repeat(jnp.exp(heights), shape[axis_at] // blocks).reshape((-1,) + (1,) * (len(shape) - axis_at - 1))

    level = one(*cuts[0])
    for cut in cuts[1:]:
        level = level * one(*cut)
    return level


def centred(stream_key, extent, scale, limit, pieces=(), kind=jnp.bfloat16):
    factor_of = level_of(stream_key, extent, pieces, -0.22, 0.18) if pieces else 1.0
    drawn = jax.random.normal(stream_key, extent, jnp.float32) * scale * factor_of
    return jnp.minimum(jnp.maximum(drawn, -limit), limit).astype(kind)


def noise_with(key, extent, width, limit, shards, heavy, kind=jnp.bfloat16):
    values = width * jax.random.normal(key, extent, jnp.float32)
    if shards:
        values = values * level_of(key, extent, shards, -0.22, 0.18)
    return jnp.clip(raised(values, jax.random.fold_in(key, 3), *heavy), -limit, limit).astype(kind)


def setup_inputs(seed: int = 0) -> dict:
    keys = jax.random.split(jax.random.key(seed), 15)
    tokens = centred(keys[0], (TOKENS, D), 1.0, 6.0, ((0, 16),))
    cotangent = noise_with(keys[1], (TOKENS, D), 1.0, 6.0, ((0, 16),), (0, 1, 16, 2.0))
    ln1_gain = jnp.clip(1.0 + 0.15 * jax.random.normal(keys[2], (D,), jnp.float32), 0.25, 1.75)
    ln1_bias = centred(keys[3], (D,), 0.3, 1.75, (), jnp.float32)
    ln2_gain = jnp.clip(1.0 + 0.15 * jax.random.normal(keys[4], (D,), jnp.float32), 0.25, 1.75)
    ln2_bias = centred(keys[5], (D,), 0.3, 1.75, (), jnp.float32)
    w_qkv = centred(keys[6], (D, 3, D), D ** -0.5, 0.1875, ((0, 4), (2, 2)))
    b_qkv = centred(keys[7], (3, D), 0.3, 1.75, ((1, 2),), jnp.float32)
    w_out = centred(keys[8], (D, D), (max(1, D * 4 // SEQ)) ** -0.5, 3.0, ((0, 4), (1, 2)))
    b_out = centred(keys[9], (D,), 0.3, 1.75, (), jnp.float32)
    w_up = centred(keys[10], (D, FF), D ** -0.5, 0.1875, ((0, 4), (1, 2)))
    b_up = centred(keys[11], (FF,), 0.3, 1.75, ((0, 2),), jnp.float32)
    w_down = centred(keys[12], (D, FF), FF ** -0.5, 0.09375, ((0, 4), (1, 2)))
    b_down = centred(keys[13], (D,), 0.3, 1.75, (), jnp.float32)
    return dict(tokens=tokens, cotangent=cotangent, ln1_gain=ln1_gain, ln1_bias=ln1_bias, ln2_gain=ln2_gain, ln2_bias=ln2_bias, w_qkv=w_qkv, b_qkv=b_qkv, w_out=w_out, b_out=b_out, w_up=w_up, b_up=b_up, w_down=w_down, b_down=b_down)


EPSILON = 1e-05
NEGATIVE = -1e+30
HIGH = lax.Precision.HIGHEST

@jax.custom_vjp
def low(v):
    return lax.optimization_barrier(v.astype(jnp.bfloat16)).astype(jnp.float32)

@jax.custom_vjp
def low_back(v):
    return v

def low_keep(v):
    return (low(v), None)

def low_pass(kept, grad):
    return (grad,)

def back_keep(v):
    return (v, None)

def back_low(kept, grad):
    return (low(grad),)
low.defvjp(low_keep, low_pass)
low_back.defvjp(back_keep, back_low)

def layer_norm(values, gain, shift):
    center = values - lax.optimization_barrier(jnp.mean(values, axis=-1, keepdims=True))
    spread = lax.optimization_barrier(jnp.mean(center * center, axis=-1, keepdims=True))
    return center * lax.rsqrt(spread + EPSILON) * gain + shift

def rotary_tables(positions, rot):
    half = rot // 2
    inverse = 1.0 / 10000.0 ** (jnp.arange(half, dtype=jnp.float32) * 2.0 / rot)
    angles = positions.astype(jnp.float32)[:, None] * inverse[None, :]
    return (jnp.cos(angles), jnp.sin(angles))

def rotate(values, cosine, sine):
    half = cosine.shape[-1]
    first = values[..., :half]
    second = values[..., half:2 * half]
    cos_b = cosine[:, None, :]
    sin_b = sine[:, None, :]
    return jnp.concatenate([first * cos_b - second * sin_b, second * cos_b + first * sin_b, values[..., 2 * half:]], axis=-1)

def attend_sequence(items):
    query, key, value = items
    size = query.shape[0]
    block = min(512, size)
    scale = 1.0 / HEAD ** 0.5
    key_pos = jnp.arange(size, dtype=jnp.int32)

    def one_block(args):
        rows_q, start = args
        raw = jnp.einsum('thd,rhd->htr', rows_q, key, precision=HIGH) * scale
        scores = low_back(raw)
        query_pos = start + jnp.arange(block, dtype=jnp.int32)
        visible = key_pos[None, None, :] <= query_pos[None, :, None]
        scores = jnp.where(visible, scores, NEGATIVE)
        top = lax.optimization_barrier(jnp.max(scores, axis=-1, keepdims=True))
        expo = jnp.where(visible, jnp.exp(scores - top), 0.0)
        total = lax.optimization_barrier(jnp.sum(expo, axis=-1, keepdims=True))
        mixed = jnp.einsum('htr,rhd->htd', low(expo), value, precision=HIGH) / total
        return mixed.transpose(1, 0, 2)
    starts = jnp.arange(size // block, dtype=jnp.int32) * block
    blocks = query.reshape(size // block, block, query.shape[1], query.shape[2])
    result = lax.map(jax.checkpoint(one_block), (blocks, starts))
    return result.reshape(size, query.shape[1], query.shape[2])

def forward(whole, gain_one, shift_one, gain_two, shift_two, w_qkv, b_qkv, w_out, b_out, w_up, b_up, w_down, b_down):
    normed_one = low(layer_norm(whole, gain_one, shift_one))
    normed_two = low(layer_norm(whole, gain_two, shift_two))
    projected = low_back(jnp.einsum('td,dke->tke', normed_one, w_qkv, precision=HIGH) + b_qkv[None])
    shaped = projected.reshape(SEQS, SEQ, 3, HEADS, HEAD)
    cosine, sine = rotary_tables(jnp.arange(SEQ, dtype=jnp.int32), ROT)
    query = low(rotate(shaped[:, :, 0], cosine, sine))
    key = low(rotate(shaped[:, :, 1], cosine, sine))
    value = low(shaped[:, :, 2])
    mixed = lax.map(attend_sequence, (query, key, value))
    mixed = low(low_back(mixed.reshape(SEQS * SEQ, D)))
    up_pre = low_back(jnp.dot(normed_two, w_up, precision=HIGH) + b_up)
    active = low(jax.nn.gelu(up_pre, approximate=False))
    branches = jnp.dot(mixed, w_out.T, precision=HIGH) + jnp.dot(active, w_down.T, precision=HIGH)
    return whole + branches + b_out + b_down

def reference(tokens, cotangent, ln1_gain, ln1_bias, ln2_gain, ln2_bias, w_qkv, b_qkv, w_out, b_out, w_up, b_up, w_down, b_down):
    inputs = tuple((item.astype(jnp.float32) for item in (tokens, ln1_gain, ln1_bias, ln2_gain, ln2_bias, w_qkv, b_qkv, w_out, b_out, w_up, b_up, w_down, b_down)))
    result, pull = jax.vjp(forward, *inputs)
    grads = pull(cotangent.astype(jnp.float32))
    return (result.astype(jnp.bfloat16), grads[0], grads[1], grads[2], grads[3], grads[4], grads[5], grads[6], grads[7], grads[8], grads[9], grads[10], grads[11], grads[12])
```

```python
import math

import jax
import jax.numpy as jnp
from jax import lax
from jax.sharding import PartitionSpec as P

HEAD = 64
ROT = 16


EPSILON = 1e-05
NEGATIVE = -1e30


def layer_norm(values, gain, shift):
    center = values - jnp.mean(values, axis=-1, keepdims=True)
    spread = jnp.mean(center * center, axis=-1, keepdims=True)
    return center * lax.rsqrt(spread + EPSILON) * gain + shift


def rotary_tables(positions, rot):
    half = rot // 2
    inverse = 1.0 / 10000.0 ** (jnp.arange(half, dtype=jnp.float32) * 2.0 / rot)
    angles = positions.astype(jnp.float32)[:, None] * inverse[None, :]
    return (jnp.cos(angles), jnp.sin(angles))


def rotate(values, cosine, sine):
    half = cosine.shape[-1]
    first = values[..., :half]
    second = values[..., half : 2 * half]
    cos_b = cosine[:, None, :]
    sin_b = sine[:, None, :]
    return jnp.concatenate(
        [first * cos_b - second * sin_b, second * cos_b + first * sin_b, values[..., 2 * half :]],
        axis=-1,
    )


def gelu_exact(values):
    return jax.nn.gelu(values, approximate=False)


def gathered_weights(
    tokens,
    cotangent,
    ln1_gain,
    ln1_bias,
    ln2_gain,
    ln2_bias,
    w_qkv,
    b_qkv,
    w_out,
    b_out,
    w_up,
    b_up,
    w_down,
    b_down,
):
    rows = tokens.shape[0]
    width = w_qkv.shape[2]
    local_heads = width // HEAD
    scale = 1.0 / math.sqrt(HEAD)
    seq_len = rows * lax.axis_size("context")
    whole = tokens.astype(jnp.float32)
    low_one = layer_norm(whole, ln1_gain, ln1_bias).astype(jnp.bfloat16)
    low_two = layer_norm(whole, ln2_gain, ln2_bias).astype(jnp.bfloat16)
    full_qkv, full_out, full_up, full_down = (
        lax.all_gather(w_qkv, "fsdp", axis=0, tiled=True),
        lax.all_gather(w_out, "fsdp", axis=0, tiled=True),
        lax.all_gather(w_up, "fsdp", axis=0, tiled=True),
        lax.all_gather(w_down, "fsdp", axis=0, tiled=True),
    )
    projected = (
        jnp.einsum("td,dke->tke", low_one, full_qkv, preferred_element_type=jnp.float32)
        + b_qkv[None]
    )
    positions = lax.axis_index("context") * rows + jnp.arange(rows, dtype=jnp.int32)
    last_query = positions[-1]
    cosine, sine = rotary_tables(positions, ROT)
    shaped = projected.reshape(rows, 3, local_heads, HEAD)
    query = rotate(shaped[:, 0], cosine, sine).astype(jnp.bfloat16)
    key = rotate(shaped[:, 1], cosine, sine).astype(jnp.bfloat16)
    value = shaped[:, 2].astype(jnp.bfloat16)
    pairs = jnp.stack([key.reshape(rows, width), value.reshape(rows, width)], axis=1)
    start_state = (
        jnp.full((local_heads, rows), NEGATIVE, jnp.float32),
        jnp.zeros((local_heads, rows), jnp.float32),
        jnp.zeros((local_heads, rows, HEAD), jnp.float32),
    )
    piece = lax.all_gather(pairs, "context", axis=0, tiled=True)
    size = piece.shape[0]
    block = math.gcd(size, math.lcm(512, rows))
    blocks = piece.reshape(size // block, block, 2, local_heads, HEAD)

    def forward_step(state, item):
        index, group = item
        first = index * block

        def forward_compute(inner):
            top, total, accum = inner
            key_pos = first + jnp.arange(block, dtype=jnp.int32)
            scores = (
                jnp.einsum("thd,rhd->htr", query, group[:, 0], preferred_element_type=jnp.float32)
                * scale
            )
            visible = key_pos[None, None, :] <= positions[None, :, None]
            scores = jnp.where(visible, scores, NEGATIVE)
            new_top = jnp.maximum(top, jnp.max(scores, axis=-1))
            weights = jnp.where(visible, jnp.exp(scores - new_top[..., None]), 0.0)
            factor = jnp.exp(top - new_top)
            total = total * factor + jnp.sum(weights, axis=-1)
            accum = accum * factor[..., None] + jnp.einsum(
                "htr,rhd->htd",
                weights.astype(jnp.bfloat16),
                group[:, 1],
                preferred_element_type=jnp.float32,
            )
            return (new_top, total, accum)

        return (lax.cond(first > last_query, lambda inner: inner, forward_compute, state), None)

    result, _ = lax.scan(
        forward_step, start_state, (jnp.arange(blocks.shape[0], dtype=jnp.int32), blocks)
    )
    top, total, accum = result
    attended = accum / total[..., None]
    log_total = top + jnp.log(total)
    mixed_low = attended.transpose(1, 0, 2).reshape(rows, width).astype(jnp.bfloat16)
    up_pre = jnp.dot(low_two, full_up, preferred_element_type=jnp.float32) + b_up
    active_low = gelu_exact(up_pre).astype(jnp.bfloat16)
    partial_sum = jnp.einsum(
        "te,de->td", mixed_low, full_out, preferred_element_type=jnp.float32
    ) + jnp.einsum("tf,df->td", active_low, full_down, preferred_element_type=jnp.float32)
    branches = lax.psum(partial_sum.astype(jnp.bfloat16), "tensor").astype(jnp.float32)
    result = (whole + branches + b_out + b_down).astype(jnp.bfloat16)
    grad_bias = jnp.sum(cotangent.astype(jnp.float32), axis=0)
    grad_w_out = jnp.einsum("td,te->de", cotangent, mixed_low, preferred_element_type=jnp.float32)
    grad_w_down = jnp.einsum("td,tf->df", cotangent, active_low, preferred_element_type=jnp.float32)
    grad_mixed = jnp.dot(cotangent, full_out, preferred_element_type=jnp.float32).astype(
        jnp.bfloat16
    )
    grad_active = jnp.dot(cotangent, full_down, preferred_element_type=jnp.float32)
    _, gelu_pull = jax.vjp(gelu_exact, up_pre)
    grad_up = gelu_pull(grad_active)[0].astype(jnp.bfloat16)
    grad_w_up = jnp.einsum("td,tf->df", low_two, grad_up, preferred_element_type=jnp.float32)
    grad_b_up = jnp.sum(grad_up.astype(jnp.float32), axis=0)
    grad_two = jnp.einsum("tf,df->td", grad_up, full_up, preferred_element_type=jnp.float32)
    grad_heads = grad_mixed.reshape(rows, local_heads, HEAD)
    delta = jnp.sum(grad_heads.astype(jnp.float32).transpose(1, 0, 2) * attended, axis=-1)
    query_start = jnp.zeros((local_heads, rows, HEAD), jnp.float32)
    back_state = (query_start, jnp.zeros((seq_len, 2, width), jnp.float32))
    piece = lax.all_gather(pairs, "context", axis=0, tiled=True)
    size = piece.shape[0]
    backward_block = math.gcd(size, math.lcm(512, rows))
    blocks = piece.reshape(size // backward_block, backward_block, 2, local_heads, HEAD)

    def backward_step(state, item):
        index, group = item
        first = index * backward_block

        def backward_compute(inner):
            grad_query = inner[0]
            key_pos = first + jnp.arange(backward_block, dtype=jnp.int32)
            scores = (
                jnp.einsum("thd,rhd->htr", query, group[:, 0], preferred_element_type=jnp.float32)
                * scale
            )
            visible = key_pos[None, None, :] <= positions[None, :, None]
            probs = jnp.where(visible, jnp.exp(scores - log_total[..., None]), 0.0)
            grad_probs = jnp.einsum(
                "thd,rhd->htr", grad_heads, group[:, 1], preferred_element_type=jnp.float32
            )
            grad_scores = (probs * (grad_probs - delta[..., None])).astype(jnp.bfloat16)
            grad_query = (
                grad_query
                + jnp.einsum(
                    "htr,rhd->htd", grad_scores, group[:, 0], preferred_element_type=jnp.float32
                )
                * scale
            )
            grad_value = jnp.einsum(
                "htr,thd->rhd",
                probs.astype(jnp.bfloat16),
                grad_heads,
                preferred_element_type=jnp.float32,
            )
            grad_key = (
                jnp.einsum("htr,thd->rhd", grad_scores, query, preferred_element_type=jnp.float32)
                * scale
            )
            update = jnp.stack(
                [
                    grad_key.reshape(backward_block, width),
                    grad_value.reshape(backward_block, width),
                ],
                axis=1,
            )
            return (grad_query, lax.dynamic_update_slice_in_dim(inner[1], update, first, 0))

        return (lax.cond(first > last_query, lambda inner: inner, backward_compute, state), None)

    result_state, _ = lax.scan(
        backward_step, back_state, (jnp.arange(blocks.shape[0], dtype=jnp.int32), blocks)
    )
    grad_query = result_state[0]
    grad_pairs = lax.psum_scatter(
        result_state[1].astype(jnp.bfloat16), "context", scatter_dimension=0, tiled=True
    ).astype(jnp.float32)
    _, turn_pull = jax.vjp(lambda values: rotate(values, cosine, sine), shaped[:, 0])
    grad_q_pre = turn_pull(grad_query.transpose(1, 0, 2))[0]
    grad_k_pre = turn_pull(grad_pairs[:, 0].reshape(rows, local_heads, HEAD))[0]
    grad_v_pre = grad_pairs[:, 1].reshape(rows, local_heads, HEAD)
    grad_proj = (
        jnp.stack([grad_q_pre, grad_k_pre, grad_v_pre], axis=1)
        .reshape(rows, 3, width)
        .astype(jnp.bfloat16)
    )
    grad_w_qkv = jnp.einsum("td,tke->dke", low_one, grad_proj, preferred_element_type=jnp.float32)
    grad_b_qkv = jnp.sum(grad_proj.astype(jnp.float32), axis=0)
    grad_one = jnp.einsum("tke,dke->td", grad_proj, full_qkv, preferred_element_type=jnp.float32)
    grad_one, grad_two = (
        lax.psum(grad_one.astype(jnp.bfloat16), "tensor").astype(jnp.float32),
        lax.psum(grad_two.astype(jnp.bfloat16), "tensor").astype(jnp.float32),
    )
    _, norm_pull_one = jax.vjp(layer_norm, whole, ln1_gain, ln1_bias)
    input_one, gain_one, shift_one = norm_pull_one(grad_one)
    _, norm_pull_two = jax.vjp(layer_norm, whole, ln2_gain, ln2_bias)
    input_two, gain_two, shift_two = norm_pull_two(grad_two)
    grad_tokens = cotangent.astype(jnp.float32) + input_one + input_two
    sum_qkv, sum_out, sum_up, sum_down, sum_g1, sum_c1, sum_g2, sum_c2, sum_bias = (
        lax.psum_scatter(grad_w_qkv, ("fsdp", "context"), scatter_dimension=0, tiled=True),
        lax.psum_scatter(grad_w_out, ("fsdp", "context"), scatter_dimension=0, tiled=True),
        lax.psum_scatter(grad_w_up, ("fsdp", "context"), scatter_dimension=0, tiled=True),
        lax.psum_scatter(grad_w_down, ("fsdp", "context"), scatter_dimension=0, tiled=True),
        lax.psum_scatter(gain_one, ("fsdp", "context"), scatter_dimension=0, tiled=True),
        lax.psum_scatter(shift_one, ("fsdp", "context"), scatter_dimension=0, tiled=True),
        lax.psum_scatter(gain_two, ("fsdp", "context"), scatter_dimension=0, tiled=True),
        lax.psum_scatter(shift_two, ("fsdp", "context"), scatter_dimension=0, tiled=True),
        lax.psum_scatter(grad_bias, ("fsdp", "context"), scatter_dimension=0, tiled=True),
    )
    bias_qkv, bias_up = lax.psum((grad_b_qkv, grad_b_up), ("fsdp", "context"))
    return (
        result,
        grad_tokens,
        sum_g1,
        sum_c1,
        sum_g2,
        sum_c2,
        sum_qkv,
        bias_qkv,
        sum_out,
        sum_bias,
        sum_up,
        bias_up,
        sum_down,
        sum_bias,
    )


def send(values, axis, step):
    size = lax.axis_size(axis)
    return lax.ppermute(values, axis, [(index, index ^ step) for index in range(size)])


def take(values, start, size, axis=0):
    return lax.dynamic_slice_in_dim(values, start, size, axis)


def put(whole, values, start, axis=0):
    return lax.dynamic_update_slice_in_dim(whole, values, start, axis)


def gather_sequence(values):
    rows = values.shape[0]
    half = rows // 2
    members = lax.axis_size("context")
    here, core = lax.axis_index("context"), lax.axis_index("tensor")
    mine = take(values, core * half, half)
    whole = jnp.zeros((rows * members, values.shape[1]), values.dtype)
    whole = put(whole, values, here * rows)
    for step in range(1, members):
        got = send(mine, "context", step)
        other = send(got, "tensor", 1)
        whole = put(whole, got, (here ^ step) * rows + core * half)
        whole = put(whole, other, (here ^ step) * rows + (1 - core) * half)
    return whole


def gather_width(values):
    rows = values.shape[0]
    members = lax.axis_size("fsdp")
    here = lax.axis_index("fsdp")
    whole = jnp.zeros((rows * members, values.shape[1]), values.dtype)
    whole = put(whole, values, here * rows)
    for step in range(1, members):
        whole = put(whole, send(values, "fsdp", step), (here ^ step) * rows)
    return whole


def sum_rows(partial):
    members = lax.axis_size("context")
    here, core = lax.axis_index("context"), lax.axis_index("tensor")
    width = partial.shape[1]
    blocks = partial.reshape(members, 2, -1, width)
    kept = lax.dynamic_index_in_dim(blocks, core, 1, keepdims=False)
    other = lax.dynamic_index_in_dim(blocks, 1 - core, 1, keepdims=False)
    kept = kept + send(other.astype(jnp.bfloat16), "tensor", 1).astype(jnp.float32)
    total = lax.dynamic_index_in_dim(kept, here, 0, keepdims=False)
    low = kept.astype(jnp.bfloat16)
    for step in range(1, members):
        piece = lax.dynamic_index_in_dim(low, here ^ step, 0, keepdims=False)
        total = total + send(piece, "context", step).astype(jnp.float32)
    return total


def both_halves(values):
    core = lax.axis_index("tensor")
    other = send(values, "tensor", 1)
    return jnp.concatenate(
        [jnp.where(core == 0, values, other), jnp.where(core == 0, other, values)], axis=0
    )


def high_low(values):
    high = values.astype(jnp.bfloat16)
    return high, (values - high.astype(jnp.float32)).astype(jnp.bfloat16)


def sum_weights(partial, biases, columns):
    members = lax.axis_size("fsdp")
    here = lax.axis_index("fsdp")
    rows = partial.shape[0] // members
    low = partial.astype(jnp.bfloat16)
    total = take(partial, here * rows, rows)
    own_bias, own_columns = biases, take(columns, here * rows, rows)
    for step in range(1, members):
        there = here ^ step
        line = jnp.concatenate([biases, take(columns, there * rows, rows)])
        line = jnp.pad(line, (0, partial.shape[1] - line.shape[0]))
        high, rest = high_low(line)
        extra = jnp.concatenate(
            [high[None], rest[None], jnp.zeros((14, line.shape[0]), jnp.bfloat16)], axis=0
        )
        got = send(
            jnp.concatenate([take(low, there * rows, rows), extra], axis=0), "fsdp", step
        ).astype(jnp.float32)
        total = total + got[:rows]
        line = got[rows] + got[rows + 1]
        own_bias = own_bias + line[: biases.shape[0]]
        own_columns = own_columns + line[biases.shape[0] : biases.shape[0] + rows]
    return total, own_bias, own_columns


def spread_weights(total, biases):
    members = lax.axis_size("context")
    here = lax.axis_index("context")
    rows = total.shape[0] // members
    width = total.shape[1]
    low = total.astype(jnp.bfloat16)
    high, rest = high_low(jnp.pad(biases, (0, width - biases.shape[0])))
    extra = jnp.concatenate(
        [high[None], rest[None], jnp.zeros((14, width), jnp.bfloat16)], axis=0
    )
    result = jnp.zeros((rows, members, width), jnp.float32)
    bias_all = jnp.zeros((members, width), jnp.float32)
    result = put(result, take(total, here * rows, rows)[:, None], here, 1)
    bias_all = put(bias_all, jnp.pad(biases, (0, width - biases.shape[0]))[None], here)
    for step in range(1, members):
        there = here ^ step
        message = jnp.concatenate([take(low, there * rows, rows), extra], axis=0)
        got = send(message, "context", step).astype(jnp.float32)
        result = put(result, got[:rows][:, None], there, 1)
        bias_all = put(bias_all, (got[rows] + got[rows + 1])[None], there)
    return result, bias_all[:, : biases.shape[0]]


def unit_values(values):
    phi = 0.5 * (1.0 + lax.erf(values * (1.0 / math.sqrt(2.0))))
    density = jnp.exp(-0.5 * values * values) * (1.0 / math.sqrt(2.0 * math.pi))
    return values * phi, phi + values * density


def matmul(first, second, contract):
    return lax.dot_general(
        first, second, ((contract[:1], contract[1:]), ((), ())), preferred_element_type=jnp.float32
    )


def whole_sequences(
    tokens,
    cotangent,
    ln1_gain,
    ln1_bias,
    ln2_gain,
    ln2_bias,
    w_qkv,
    b_qkv,
    w_out,
    b_out,
    w_up,
    b_up,
    w_down,
    b_down,
):
    members = lax.axis_size("context")
    here, core = lax.axis_index("context"), lax.axis_index("tensor")
    rows, depth = tokens.shape
    width = w_qkv.shape[2] // members
    units = w_up.shape[1] // members
    heads = width // HEAD
    seq_len = rows * members
    scale = 1.0 / math.sqrt(HEAD)

    own_qkv = take(w_qkv, here * width, width, 2).reshape(-1, 3 * width)
    own_up = take(w_up, here * units, units, 1)
    own_back = jnp.concatenate(
        [take(w_out, here * width, width, 1), take(w_down, here * units, units, 1)], axis=1
    )
    seq = gather_sequence(tokens)
    full_qkv = gather_width(own_qkv)
    full_up = gather_width(own_up)
    full_back = gather_width(own_back)
    grad = gather_sequence(cotangent)

    seq = seq.astype(jnp.float32)
    center = seq - jnp.mean(seq, axis=-1, keepdims=True)
    spread = jnp.mean(center * center, axis=-1, keepdims=True)
    normed = center * lax.rsqrt(spread + EPSILON)
    low_one = (normed * ln1_gain + ln1_bias).astype(jnp.bfloat16)
    low_two = (normed * ln2_gain + ln2_bias).astype(jnp.bfloat16)
    normed = normed.astype(jnp.bfloat16)

    bias = take(b_qkv, here * width, width, 1).reshape(1, 3 * width)
    projected = matmul(low_one, full_qkv, (1, 0)) + bias
    cosine, sine = rotary_tables(jnp.arange(seq_len, dtype=jnp.int32), ROT)
    shaped = projected.reshape(seq_len, 3, heads, HEAD)
    query = rotate(shaped[:, 0], cosine, sine).astype(jnp.bfloat16)
    key = rotate(shaped[:, 1], cosine, sine).astype(jnp.bfloat16)
    value = shaped[:, 2].astype(jnp.bfloat16)
    scores = jnp.einsum("thd,rhd->htr", query, key, preferred_element_type=jnp.float32) * scale
    where = jnp.arange(seq_len)
    visible = where[None, None, :] <= where[None, :, None]
    scores = jnp.where(visible, scores, NEGATIVE)
    top = jnp.max(scores, axis=-1, keepdims=True)
    weights = jnp.where(visible, jnp.exp(scores - top), 0.0)
    total = jnp.sum(weights, axis=-1, keepdims=True)
    mixed = (
        jnp.einsum(
            "htr,rhd->htd", weights.astype(jnp.bfloat16), value, preferred_element_type=jnp.float32
        )
        / total
    )
    mixed_low = mixed.transpose(1, 0, 2).reshape(seq_len, width).astype(jnp.bfloat16)
    up_pre = matmul(low_two, full_up, (1, 0)) + take(b_up, here * units, units)
    active, slope = unit_values(up_pre)
    joined = jnp.concatenate([mixed_low, active.astype(jnp.bfloat16)], axis=1)
    branches = sum_rows(matmul(joined, full_back, (1, 1)))

    half = rows // 2
    own = take(tokens, core * half, half).astype(jnp.float32)
    result = both_halves((own + branches + b_out + b_down).astype(jnp.bfloat16))

    grad_joined = matmul(grad, full_back, (1, 0))
    grad_heads = grad_joined[:, :width].astype(jnp.bfloat16).reshape(seq_len, heads, HEAD)
    grad_up = (grad_joined[:, width:] * slope).astype(jnp.bfloat16)
    delta = jnp.sum(grad_heads.astype(jnp.float32).transpose(1, 0, 2) * mixed, axis=-1)
    probs = weights / total
    grad_probs = jnp.einsum("thd,rhd->htr", grad_heads, value, preferred_element_type=jnp.float32)
    grad_scores = (probs * (grad_probs - delta[..., None])).astype(jnp.bfloat16)
    grad_query = (
        jnp.einsum("htr,rhd->thd", grad_scores, key, preferred_element_type=jnp.float32) * scale
    )
    grad_key = (
        jnp.einsum("htr,thd->rhd", grad_scores, query, preferred_element_type=jnp.float32) * scale
    )
    grad_value = jnp.einsum(
        "htr,thd->rhd", probs.astype(jnp.bfloat16), grad_heads, preferred_element_type=jnp.float32
    )
    grad_proj = jnp.stack(
        [rotate(grad_query, cosine, -sine), rotate(grad_key, cosine, -sine), grad_value], axis=1
    )
    grad_proj = grad_proj.reshape(seq_len, 3 * width).astype(jnp.bfloat16)
    grad_first = jnp.concatenate([grad_proj, grad_up], axis=1)

    grad_w = jnp.concatenate(
        [matmul(normed, grad_first, (0, 0)), matmul(grad, joined, (0, 0))], axis=1
    )
    biases = jnp.sum(grad_first.astype(jnp.float32), axis=0)
    columns = jnp.sum(grad.astype(jnp.float32), axis=0)
    grad_w, biases, columns = sum_weights(grad_w, biases, columns)
    grad_w, biases = spread_weights(grad_w, biases)

    grad_norm = (
        matmul(grad_proj, full_qkv, (1, 1)) * ln1_gain + matmul(grad_up, full_up, (1, 1)) * ln2_gain
    )
    grad_norm = sum_rows(grad_norm)
    center = own - jnp.mean(own, axis=-1, keepdims=True)
    factor = lax.rsqrt(jnp.mean(center * center, axis=-1, keepdims=True) + EPSILON)
    hat = center * factor
    grad_input = factor * (
        grad_norm
        - jnp.mean(grad_norm, axis=-1, keepdims=True)
        - hat * jnp.mean(grad_norm * hat, axis=-1, keepdims=True)
    )
    own_grad = take(cotangent, core * half, half).astype(jnp.float32)
    grad_tokens = both_halves(own_grad + grad_input)

    lines = grad_w.shape[0]
    first = lax.axis_index("fsdp") * (depth // lax.axis_size("fsdp")) + here * lines
    gain_one, shift_one = take(ln1_gain, first, lines), take(ln1_bias, first, lines)
    gain_two, shift_two = take(ln2_gain, first, lines), take(ln2_bias, first, lines)
    hat_qkv = grad_w[:, :, : 3 * width].reshape(lines, members, 3, width)
    hat_qkv = hat_qkv.transpose(0, 2, 1, 3).reshape(lines, 3, members * width)
    cut = 3 * width + units
    hat_up = grad_w[:, :, 3 * width : cut].reshape(lines, members * units)
    grad_w_out = grad_w[:, :, cut : cut + width].reshape(lines, members * width)
    grad_w_down = grad_w[:, :, cut + width :].reshape(lines, members * units)
    bias_qkv = biases[:, : 3 * width].reshape(members, 3, width).transpose(1, 0, 2)
    bias_qkv = bias_qkv.reshape(3, members * width)
    bias_up = biases[:, 3 * width :].reshape(members * units)
    grad_w_qkv = hat_qkv * gain_one[:, None, None] + shift_one[:, None, None] * bias_qkv[None]
    grad_w_up = hat_up * gain_two[:, None] + shift_two[:, None] * bias_up[None]
    here_qkv = take(w_qkv, here * lines, lines).astype(jnp.float32)
    here_up = take(w_up, here * lines, lines).astype(jnp.float32)
    norms = jnp.stack(
        [
            jnp.sum(here_qkv * hat_qkv, axis=(1, 2)),
            jnp.sum(here_qkv * bias_qkv[None], axis=(1, 2)),
            jnp.sum(here_up * hat_up, axis=1),
            jnp.sum(here_up * bias_up[None], axis=1),
        ]
    )
    norms = norms + send(norms, "tensor", 1)
    columns = take(columns, here * lines, lines)
    return (
        result,
        grad_tokens,
        norms[0],
        norms[1],
        norms[2],
        norms[3],
        grad_w_qkv,
        bias_qkv,
        grad_w_out,
        columns,
        grad_w_up,
        bias_up,
        grad_w_down,
        columns,
    )


def power_of_two(number):
    return number & (number - 1) == 0


def on_device(*arrays):
    members = lax.axis_size("context")
    local_heads = arrays[6].shape[2] // HEAD
    units = arrays[10].shape[1]
    fits = (
        local_heads % members == 0
        and units % members == 0
        and lax.axis_size("tensor") == 2
        and power_of_two(members)
        and power_of_two(lax.axis_size("fsdp"))
    )
    return whole_sequences(*arrays) if fits else gathered_weights(*arrays)


def solution(mesh):
    in_specs = (
        P(("fsdp", "context"), None),
        P(("fsdp", "context"), None),
        P(),
        P(),
        P(),
        P(),
        P("fsdp", None, "tensor"),
        P(None, "tensor"),
        P("fsdp", "tensor"),
        P(),
        P("fsdp", "tensor"),
        P("tensor"),
        P("fsdp", "tensor"),
        P(),
    )
    out_specs = (
        P(("fsdp", "context"), None),
        P(("fsdp", "context"), None),
        P(("fsdp", "context")),
        P(("fsdp", "context")),
        P(("fsdp", "context")),
        P(("fsdp", "context")),
        P(("fsdp", "context"), None, "tensor"),
        P(None, "tensor"),
        P(("fsdp", "context"), "tensor"),
        P(("fsdp", "context")),
        P(("fsdp", "context"), "tensor"),
        P("tensor"),
        P(("fsdp", "context"), "tensor"),
        P(("fsdp", "context")),
    )
    return jax.shard_map(
        on_device, mesh=mesh, in_specs=in_specs, out_specs=out_specs, check_vma=False
    )
```

```python
import math

import jax
import jax.numpy as jnp
from jax import lax
from jax.experimental import pallas as pl
from jax.experimental.pallas import tpu as pltpu
from jax.sharding import PartitionSpec as P

HEAD = 64
ROT = 16


EPSILON = 1e-05
NEGATIVE = -1e30


def layer_norm(values, gain, shift):
    center = values - jnp.mean(values, axis=-1, keepdims=True)
    spread = jnp.mean(center * center, axis=-1, keepdims=True)
    return center * lax.rsqrt(spread + EPSILON) * gain + shift


def rotary_tables(positions, rot):
    half = rot // 2
    inverse = 1.0 / 10000.0 ** (jnp.arange(half, dtype=jnp.float32) * 2.0 / rot)
    angles = positions.astype(jnp.float32)[:, None] * inverse[None, :]
    return (jnp.cos(angles), jnp.sin(angles))


def rotate(values, cosine, sine):
    half = cosine.shape[-1]
    first = values[..., :half]
    second = values[..., half : 2 * half]
    cos_b = cosine[:, None, :]
    sin_b = sine[:, None, :]
    return jnp.concatenate(
        [first * cos_b - second * sin_b, second * cos_b + first * sin_b, values[..., 2 * half :]],
        axis=-1,
    )


def gelu_exact(values):
    return jax.nn.gelu(values, approximate=False)


def gathered_weights(
    tokens,
    cotangent,
    ln1_gain,
    ln1_bias,
    ln2_gain,
    ln2_bias,
    w_qkv,
    b_qkv,
    w_out,
    b_out,
    w_up,
    b_up,
    w_down,
    b_down,
):
    rows = tokens.shape[0]
    width = w_qkv.shape[2]
    local_heads = width // HEAD
    scale = 1.0 / math.sqrt(HEAD)
    seq_len = rows * lax.axis_size("context")
    whole = tokens.astype(jnp.float32)
    low_one = layer_norm(whole, ln1_gain, ln1_bias).astype(jnp.bfloat16)
    low_two = layer_norm(whole, ln2_gain, ln2_bias).astype(jnp.bfloat16)
    full_qkv, full_out, full_up, full_down = (
        lax.all_gather(w_qkv, "fsdp", axis=0, tiled=True),
        lax.all_gather(w_out, "fsdp", axis=0, tiled=True),
        lax.all_gather(w_up, "fsdp", axis=0, tiled=True),
        lax.all_gather(w_down, "fsdp", axis=0, tiled=True),
    )
    projected = (
        jnp.einsum("td,dke->tke", low_one, full_qkv, preferred_element_type=jnp.float32)
        + b_qkv[None]
    )
    positions = lax.axis_index("context") * rows + jnp.arange(rows, dtype=jnp.int32)
    last_query = positions[-1]
    cosine, sine = rotary_tables(positions, ROT)
    shaped = projected.reshape(rows, 3, local_heads, HEAD)
    query = rotate(shaped[:, 0], cosine, sine).astype(jnp.bfloat16)
    key = rotate(shaped[:, 1], cosine, sine).astype(jnp.bfloat16)
    value = shaped[:, 2].astype(jnp.bfloat16)
    pairs = jnp.stack([key.reshape(rows, width), value.reshape(rows, width)], axis=1)
    start_state = (
        jnp.full((local_heads, rows), NEGATIVE, jnp.float32),
        jnp.zeros((local_heads, rows), jnp.float32),
        jnp.zeros((local_heads, rows, HEAD), jnp.float32),
    )
    piece = lax.all_gather(pairs, "context", axis=0, tiled=True)
    size = piece.shape[0]
    block = math.gcd(size, math.lcm(512, rows))
    blocks = piece.reshape(size // block, block, 2, local_heads, HEAD)

    def forward_step(state, item):
        index, group = item
        first = index * block

        def forward_compute(inner):
            top, total, accum = inner
            key_pos = first + jnp.arange(block, dtype=jnp.int32)
            scores = (
                jnp.einsum("thd,rhd->htr", query, group[:, 0], preferred_element_type=jnp.float32)
                * scale
            )
            visible = key_pos[None, None, :] <= positions[None, :, None]
            scores = jnp.where(visible, scores, NEGATIVE)
            new_top = jnp.maximum(top, jnp.max(scores, axis=-1))
            weights = jnp.where(visible, jnp.exp(scores - new_top[..., None]), 0.0)
            factor = jnp.exp(top - new_top)
            total = total * factor + jnp.sum(weights, axis=-1)
            accum = accum * factor[..., None] + jnp.einsum(
                "htr,rhd->htd",
                weights.astype(jnp.bfloat16),
                group[:, 1],
                preferred_element_type=jnp.float32,
            )
            return (new_top, total, accum)

        return (lax.cond(first > last_query, lambda inner: inner, forward_compute, state), None)

    result, _ = lax.scan(
        forward_step, start_state, (jnp.arange(blocks.shape[0], dtype=jnp.int32), blocks)
    )
    top, total, accum = result
    attended = accum / total[..., None]
    log_total = top + jnp.log(total)
    mixed_low = attended.transpose(1, 0, 2).reshape(rows, width).astype(jnp.bfloat16)
    up_pre = jnp.dot(low_two, full_up, preferred_element_type=jnp.float32) + b_up
    active_low = gelu_exact(up_pre).astype(jnp.bfloat16)
    partial_sum = jnp.einsum(
        "te,de->td", mixed_low, full_out, preferred_element_type=jnp.float32
    ) + jnp.einsum("tf,df->td", active_low, full_down, preferred_element_type=jnp.float32)
    branches = lax.psum(partial_sum.astype(jnp.bfloat16), "tensor").astype(jnp.float32)
    result = (whole + branches + b_out + b_down).astype(jnp.bfloat16)
    grad_bias = jnp.sum(cotangent.astype(jnp.float32), axis=0)
    grad_w_out = jnp.einsum("td,te->de", cotangent, mixed_low, preferred_element_type=jnp.float32)
    grad_w_down = jnp.einsum("td,tf->df", cotangent, active_low, preferred_element_type=jnp.float32)
    grad_mixed = jnp.dot(cotangent, full_out, preferred_element_type=jnp.float32).astype(
        jnp.bfloat16
    )
    grad_active = jnp.dot(cotangent, full_down, preferred_element_type=jnp.float32)
    _, gelu_pull = jax.vjp(gelu_exact, up_pre)
    grad_up = gelu_pull(grad_active)[0].astype(jnp.bfloat16)
    grad_w_up = jnp.einsum("td,tf->df", low_two, grad_up, preferred_element_type=jnp.float32)
    grad_b_up = jnp.sum(grad_up.astype(jnp.float32), axis=0)
    grad_two = jnp.einsum("tf,df->td", grad_up, full_up, preferred_element_type=jnp.float32)
    grad_heads = grad_mixed.reshape(rows, local_heads, HEAD)
    delta = jnp.sum(grad_heads.astype(jnp.float32).transpose(1, 0, 2) * attended, axis=-1)
    query_start = jnp.zeros((local_heads, rows, HEAD), jnp.float32)
    back_state = (query_start, jnp.zeros((seq_len, 2, width), jnp.float32))
    piece = lax.all_gather(pairs, "context", axis=0, tiled=True)
    size = piece.shape[0]
    backward_block = math.gcd(size, math.lcm(512, rows))
    blocks = piece.reshape(size // backward_block, backward_block, 2, local_heads, HEAD)

    def backward_step(state, item):
        index, group = item
        first = index * backward_block

        def backward_compute(inner):
            grad_query = inner[0]
            key_pos = first + jnp.arange(backward_block, dtype=jnp.int32)
            scores = (
                jnp.einsum("thd,rhd->htr", query, group[:, 0], preferred_element_type=jnp.float32)
                * scale
            )
            visible = key_pos[None, None, :] <= positions[None, :, None]
            probs = jnp.where(visible, jnp.exp(scores - log_total[..., None]), 0.0)
            grad_probs = jnp.einsum(
                "thd,rhd->htr", grad_heads, group[:, 1], preferred_element_type=jnp.float32
            )
            grad_scores = (probs * (grad_probs - delta[..., None])).astype(jnp.bfloat16)
            grad_query = (
                grad_query
                + jnp.einsum(
                    "htr,rhd->htd", grad_scores, group[:, 0], preferred_element_type=jnp.float32
                )
                * scale
            )
            grad_value = jnp.einsum(
                "htr,thd->rhd",
                probs.astype(jnp.bfloat16),
                grad_heads,
                preferred_element_type=jnp.float32,
            )
            grad_key = (
                jnp.einsum("htr,thd->rhd", grad_scores, query, preferred_element_type=jnp.float32)
                * scale
            )
            update = jnp.stack(
                [
                    grad_key.reshape(backward_block, width),
                    grad_value.reshape(backward_block, width),
                ],
                axis=1,
            )
            return (grad_query, lax.dynamic_update_slice_in_dim(inner[1], update, first, 0))

        return (lax.cond(first > last_query, lambda inner: inner, backward_compute, state), None)

    result_state, _ = lax.scan(
        backward_step, back_state, (jnp.arange(blocks.shape[0], dtype=jnp.int32), blocks)
    )
    grad_query = result_state[0]
    grad_pairs = lax.psum_scatter(
        result_state[1].astype(jnp.bfloat16), "context", scatter_dimension=0, tiled=True
    ).astype(jnp.float32)
    _, turn_pull = jax.vjp(lambda values: rotate(values, cosine, sine), shaped[:, 0])
    grad_q_pre = turn_pull(grad_query.transpose(1, 0, 2))[0]
    grad_k_pre = turn_pull(grad_pairs[:, 0].reshape(rows, local_heads, HEAD))[0]
    grad_v_pre = grad_pairs[:, 1].reshape(rows, local_heads, HEAD)
    grad_proj = (
        jnp.stack([grad_q_pre, grad_k_pre, grad_v_pre], axis=1)
        .reshape(rows, 3, width)
        .astype(jnp.bfloat16)
    )
    grad_w_qkv = jnp.einsum("td,tke->dke", low_one, grad_proj, preferred_element_type=jnp.float32)
    grad_b_qkv = jnp.sum(grad_proj.astype(jnp.float32), axis=0)
    grad_one = jnp.einsum("tke,dke->td", grad_proj, full_qkv, preferred_element_type=jnp.float32)
    grad_one, grad_two = (
        lax.psum(grad_one.astype(jnp.bfloat16), "tensor").astype(jnp.float32),
        lax.psum(grad_two.astype(jnp.bfloat16), "tensor").astype(jnp.float32),
    )
    _, norm_pull_one = jax.vjp(layer_norm, whole, ln1_gain, ln1_bias)
    input_one, gain_one, shift_one = norm_pull_one(grad_one)
    _, norm_pull_two = jax.vjp(layer_norm, whole, ln2_gain, ln2_bias)
    input_two, gain_two, shift_two = norm_pull_two(grad_two)
    grad_tokens = cotangent.astype(jnp.float32) + input_one + input_two
    sum_qkv, sum_out, sum_up, sum_down, sum_g1, sum_c1, sum_g2, sum_c2, sum_bias = (
        lax.psum_scatter(grad_w_qkv, ("fsdp", "context"), scatter_dimension=0, tiled=True),
        lax.psum_scatter(grad_w_out, ("fsdp", "context"), scatter_dimension=0, tiled=True),
        lax.psum_scatter(grad_w_up, ("fsdp", "context"), scatter_dimension=0, tiled=True),
        lax.psum_scatter(grad_w_down, ("fsdp", "context"), scatter_dimension=0, tiled=True),
        lax.psum_scatter(gain_one, ("fsdp", "context"), scatter_dimension=0, tiled=True),
        lax.psum_scatter(shift_one, ("fsdp", "context"), scatter_dimension=0, tiled=True),
        lax.psum_scatter(gain_two, ("fsdp", "context"), scatter_dimension=0, tiled=True),
        lax.psum_scatter(shift_two, ("fsdp", "context"), scatter_dimension=0, tiled=True),
        lax.psum_scatter(grad_bias, ("fsdp", "context"), scatter_dimension=0, tiled=True),
    )
    bias_qkv, bias_up = lax.psum((grad_b_qkv, grad_b_up), ("fsdp", "context"))
    return (
        result,
        grad_tokens,
        sum_g1,
        sum_c1,
        sum_g2,
        sum_c2,
        sum_qkv,
        bias_qkv,
        sum_out,
        sum_bias,
        sum_up,
        bias_up,
        sum_down,
        sum_bias,
    )


VMEM_BYTES = 60 * 1024 * 1024


def send(values, axis, step):
    size = lax.axis_size(axis)
    return lax.ppermute(values, axis, [(index, index ^ step) for index in range(size)])


def take(values, start, size, axis=0):
    return lax.dynamic_slice_in_dim(values, start, size, axis)


def both_halves(values):
    core = lax.axis_index("tensor")
    other = send(values, "tensor", 1)
    return jnp.concatenate(
        [jnp.where(core == 0, values, other), jnp.where(core == 0, other, values)], axis=0
    )


def call(body, outs, place, *arrays, scratch=()):
    return pl.pallas_call(
        body,
        out_shape=[jax.ShapeDtypeStruct(shape, kind) for shape, kind in outs],
        in_specs=[pl.BlockSpec(memory_space=pltpu.SMEM)]
        + [pl.BlockSpec(memory_space=pltpu.VMEM)] * len(arrays),
        out_specs=[pl.BlockSpec(memory_space=pltpu.VMEM)] * len(outs),
        scratch_shapes=[pltpu.VMEM(shape, kind) for shape, kind in scratch],
        compiler_params=pltpu.CompilerParams(vmem_limit_bytes=VMEM_BYTES),
    )(place, *arrays)


def span(index, size, offset=0):
    return pl.ds(pl.multiple_of(index * size + offset, size), size)


def dot(first, second, contract=(1, 0)):
    return lax.dot_general(
        first, second, ((contract[:1], contract[1:]), ((), ())), preferred_element_type=jnp.float32
    )


def high_low(values):
    high = values.astype(jnp.bfloat16)
    return high, (values - high.astype(jnp.float32)).astype(jnp.bfloat16)


def small_rows(lines, width):
    rows = []
    for line in lines:
        rest = width - line.shape[1]
        if rest:
            line = jnp.concatenate([line, jnp.zeros((1, rest), jnp.float32)], axis=1)
        rows.extend(high_low(line))
    rows.append(jnp.zeros((16 - len(rows), width), jnp.bfloat16))
    return jnp.concatenate([row.astype(jnp.float32) for row in rows], axis=0).astype(jnp.bfloat16)


def turn(values, table, sign):
    wide = values.shape[1]
    half = ROT // 2
    ahead = pltpu.roll(values, wide - half, 1)
    behind = pltpu.roll(values, half, 1)
    return values * table[0] + sign * (ahead * table[1] + behind * table[2])


def turn_tables(seq_len, width):
    cosine, sine = rotary_tables(jnp.arange(seq_len, dtype=jnp.int32), ROT)
    rest = jnp.zeros((seq_len, HEAD - ROT), jnp.float32)
    none = jnp.zeros_like(sine)
    one = jnp.concatenate([cosine, cosine, rest + 1.0], axis=1)
    ahead = jnp.concatenate([-sine, none, rest], axis=1)
    behind = jnp.concatenate([none, sine, rest], axis=1)
    heads = width // HEAD
    return jnp.stack([jnp.tile(part, (1, heads)) for part in (one, ahead, behind)])


def pack_kernel(place, tokens, cotangent, qkv, out, up, down, half_tokens, half_grad, first, second):
    here, core = place[1], place[2]
    rows = half_tokens.shape[0]
    half_tokens[...] = tokens[span(core, rows), :]
    half_grad[...] = cotangent[span(core, rows), :]
    width = (first.shape[1] - second.shape[1]) // 2
    units = second.shape[1] - width
    for part in range(3):
        first[:, part * width : (part + 1) * width] = qkv[:, part, span(here, width)]
    first[:, 3 * width :] = up[:, span(here, units)]
    second[:, :width] = out[:, span(here, width)]
    second[:, width:] = down[:, span(here, units)]


def assemble_rows(place, whole, own, got, other):
    here, core = place[1], place[2]
    rows, half = own.shape[0], own.shape[0] // 2
    whole[span(here, rows), :] = own[...]
    for step in range(1, len(got) + 1):
        start = (here ^ step) * rows
        whole[pl.ds(pl.multiple_of(start + core * half, half), half), :] = got[step - 1][...]
        whole[pl.ds(pl.multiple_of(start + (1 - core) * half, half), half), :] = other[step - 1][...]


def assemble_width(place, whole, parts):
    rows = parts[0].shape[0]
    for step, part in enumerate(parts):
        whole[span(place[0] ^ step, rows), :] = part[...]


def head_mask(width, head):
    lane = lax.broadcasted_iota(jnp.int32, (1, width), 1)
    return (lane >= head * HEAD) & (lane < (head + 1) * HEAD)


def only_head(values, head):
    return jnp.where(head_mask(values.shape[1], head), values, jnp.zeros_like(values))


def causal(block, keys):
    row = lax.broadcasted_iota(jnp.int32, (block, keys), 0) + (keys - block)
    return lax.broadcasted_iota(jnp.int32, (block, keys), 1) <= row


def forward_kernel(members, quarters, place, *refs):
    own, refs = refs[0], refs[1:]
    got, refs = refs[: members - 1], refs[members - 1 :]
    other, refs = refs[: members - 1], refs[members - 1 :]
    parts, refs = refs[:quarters], refs[quarters:]
    gain_one, shift_one, gain_two, shift_two, bias_qkv, bias_up, table = refs[:7]
    hat, qkv, mixed, log_total, joined, slope, weights, seq = refs[7:]
    assemble_rows(place, seq, own, got, other)
    assemble_width(place, weights, parts)
    seq_len = seq.shape[0]
    width = mixed.shape[1]
    block = own.shape[0]
    for start in range(0, seq_len, block):
        rows = slice(start, start + block)
        values = seq[rows, :].astype(jnp.float32)
        center = values - jnp.mean(values, axis=-1, keepdims=True)
        spread = jnp.mean(center * center, axis=-1, keepdims=True)
        normed = center * lax.rsqrt(spread + EPSILON)
        hat[rows, :] = normed.astype(jnp.bfloat16)
        low_one = (normed * gain_one[...] + shift_one[...]).astype(jnp.bfloat16)
        projected = dot(low_one, weights[:, : 3 * width]) + bias_qkv[...]
        turning = [table[part, rows, :] for part in range(3)]
        query = turn(projected[:, :width], turning, 1.0).astype(jnp.bfloat16)
        qkv[rows, :width] = query * (1.0 / math.sqrt(HEAD))
        qkv[rows, width : 2 * width] = turn(
            projected[:, width : 2 * width], turning, 1.0
        ).astype(jnp.bfloat16)
        qkv[rows, 2 * width :] = projected[:, 2 * width :].astype(jnp.bfloat16)
        low_two = (normed * gain_two[...] + shift_two[...]).astype(jnp.bfloat16)
        pre = dot(low_two, weights[:, 3 * width :]) + bias_up[...]
        phi = 0.5 * (1.0 + lax.erf(pre * (1.0 / math.sqrt(2.0))))
        density = jnp.exp(-0.5 * pre * pre) * (1.0 / math.sqrt(2.0 * math.pi))
        joined[rows, width:] = (pre * phi).astype(jnp.bfloat16)
        slope[rows, :] = phi + pre * density
    for start in range(0, seq_len, block):
        rows = slice(start, start + block)
        keys = start + block
        visible = causal(block, keys)
        result = jnp.zeros((block, width), jnp.float32)
        logs = jnp.zeros((block, width), jnp.float32)
        for head in range(width // HEAD):
            scores = dot(only_head(qkv[rows, :width], head), qkv[:keys, width : 2 * width], (1, 1))
            scores = jnp.where(visible, scores, NEGATIVE)
            top = jnp.max(scores, axis=-1, keepdims=True)
            expo = jnp.where(visible, jnp.exp(scores - top), 0.0)
            total = jnp.sum(expo, axis=-1, keepdims=True)
            attended = dot(expo.astype(jnp.bfloat16), qkv[:keys, 2 * width :]) / total
            mask = head_mask(width, head)
            result = jnp.where(mask, attended, result)
            logs = jnp.where(mask, top + jnp.log(total), logs)
        mixed[rows, :] = result
        log_total[rows, :] = logs
        joined[rows, :width] = result.astype(jnp.bfloat16)


def branch_kernel(members, place, joined, *refs):
    parts, (weights, kept, other) = refs[:-3], refs[-3:]
    assemble_width(place, weights, parts)
    here, core = place[1], place[2]
    half = kept.shape[1]
    for step in range(members):
        start = (here ^ step) * (2 * half)
        mine = joined[pl.ds(pl.multiple_of(start + core * half, half), half), :]
        kept[step] = dot(mine, weights[...], (1, 1))
        twin = joined[pl.ds(pl.multiple_of(start + (1 - core) * half, half), half), :]
        other[step] = dot(twin, weights[...], (1, 1)).astype(jnp.bfloat16)


def gradient_kernel(members, quarters, place, own, *refs):
    got, refs = refs[: members - 1], refs[members - 1 :]
    other, refs = refs[: members - 1], refs[members - 1 :]
    hat, joined, slope, weights = refs[:4]
    messages, (grad_heads, grad_up, grad) = refs[4 : 4 + quarters], refs[4 + quarters :]
    assemble_rows(place, grad, own, got, other)
    seq_len, depth = grad.shape
    width = grad_heads.shape[1]
    units = grad_up.shape[1]
    block = own.shape[0]
    biases = jnp.zeros((1, units), jnp.float32)
    for start in range(0, seq_len, block):
        rows = slice(start, start + block)
        back = dot(grad[rows, :], weights[...])
        grad_heads[rows, :] = back[:, :width].astype(jnp.bfloat16)
        low = (back[:, width:] * slope[rows, :]).astype(jnp.bfloat16)
        grad_up[rows, :] = low
        biases = biases + jnp.sum(low.astype(jnp.float32), axis=0, keepdims=True)
    part = depth // quarters
    for step in range(quarters):
        columns = span(place[0] ^ step, part)
        message = messages[step]
        message[:part, :units] = dot(hat[:, columns], grad_up[...], (0, 0)).astype(jnp.bfloat16)
        values = grad[:, columns]
        message[:part, units:] = dot(values, joined[...], (0, 0)).astype(jnp.bfloat16)
        sums = jnp.sum(values.astype(jnp.float32), axis=0, keepdims=True)
        message[part:, :] = small_rows([biases, sums], message.shape[1])


def backward_kernel(members, quarters, place, *refs):
    qkv, mixed, log_total, grad_heads, grad_up, hat, weights, table, gain_one, gain_two = refs[:10]
    kept, other = refs[10:12]
    messages, (grad_proj, sum_key, sum_value) = refs[12 : 12 + quarters], refs[12 + quarters :]
    here, core = place[1], place[2]
    seq_len, width = mixed.shape
    half = kept.shape[1]
    block = 2 * half
    scale = 1.0 / math.sqrt(HEAD)
    sum_key[...] = jnp.zeros_like(sum_key)
    sum_value[...] = jnp.zeros_like(sum_value)
    for start in range(0, seq_len, block):
        rows = slice(start, start + block)
        keys = start + block
        visible = causal(block, keys)
        key, value = qkv[:keys, width : 2 * width], qkv[:keys, 2 * width :]
        grad_query = jnp.zeros((block, width), jnp.float32)
        grad_key = jnp.zeros((keys, width), jnp.float32)
        grad_value = jnp.zeros((keys, width), jnp.float32)
        product = grad_heads[rows, :].astype(jnp.float32) * mixed[rows, :]
        for head in range(width // HEAD):
            query = only_head(qkv[rows, :width], head)
            heads = only_head(grad_heads[rows, :], head)
            delta = jnp.sum(only_head(product, head), axis=-1, keepdims=True)
            logs = log_total[rows, head * HEAD : head * HEAD + 1]
            scores = dot(query, key, (1, 1))
            probs = jnp.where(visible, jnp.exp(scores - logs), 0.0)
            grad_scores = (probs * (dot(heads, value, (1, 1)) - delta)).astype(jnp.bfloat16)
            grad_query = jnp.where(
                head_mask(width, head), dot(grad_scores, key) * scale, grad_query
            )
            grad_key = grad_key + dot(grad_scores, query, (0, 0))
            grad_value = grad_value + dot(probs.astype(jnp.bfloat16), heads, (0, 0))
        turning = [table[part, rows, :] for part in range(3)]
        grad_proj[rows, :width] = turn(grad_query, turning, -1.0).astype(jnp.bfloat16)
        sum_key[:keys, :] += grad_key
        sum_value[:keys, :] += grad_value
    for start in range(0, seq_len, block):
        rows = slice(start, start + block)
        turning = [table[part, rows, :] for part in range(3)]
        grad_proj[rows, width : 2 * width] = turn(sum_key[rows, :], turning, -1.0).astype(
            jnp.bfloat16
        )
        grad_proj[rows, 2 * width :] = sum_value[rows, :].astype(jnp.bfloat16)

    def norm_gradient(rows):
        return (
            dot(grad_proj[rows, :], weights[:, : 3 * width], (1, 1)) * gain_one[...]
            + dot(grad_up[rows, :], weights[:, 3 * width :], (1, 1)) * gain_two[...]
        )

    for step in range(members):
        start = (here ^ step) * block
        kept[step] = norm_gradient(pl.ds(pl.multiple_of(start + core * half, half), half))
        twin = norm_gradient(pl.ds(pl.multiple_of(start + (1 - core) * half, half), half))
        other[step] = twin.astype(jnp.bfloat16)
    depth = hat.shape[1]
    part = depth // quarters
    biases = jnp.sum(grad_proj[...].astype(jnp.float32), axis=0, keepdims=True)
    for step in range(quarters):
        message = messages[step]
        message[:part, :] = dot(
            hat[:, span(place[0] ^ step, part)], grad_proj[...], (0, 0)
        ).astype(jnp.bfloat16)
        message[part:, :] = small_rows([biases], message.shape[1])


def share_kernel(members, quarters, place, *refs):
    parts, messages, line = refs[:quarters], refs[quarters : quarters + members], refs[-1]
    rows = messages[0].shape[0] - 16
    whole = rows * members
    for step in range(members):
        chosen = span(place[1] ^ step, rows)
        total = parts[0][chosen, :].astype(jnp.float32)
        for part in parts[1:]:
            total = total + part[chosen, :].astype(jnp.float32)
        messages[step][:rows, :] = total.astype(jnp.bfloat16)
    total = parts[0][whole:, :].astype(jnp.float32)
    for part in parts[1:]:
        total = total + part[whole:, :].astype(jnp.float32)
    lines = [total[2 * index : 2 * index + 1] + total[2 * index + 1 : 2 * index + 2] for index in (0, 1)]
    line[...] = lines[1]
    small = small_rows(lines[:1], total.shape[1])
    for step in range(members):
        messages[step][rows:, :] = small


def owner_kernel(members, place, *refs):
    first, refs = refs[:members], refs[members:]
    second, refs = refs[:members], refs[members:]
    w_qkv, w_up, gain_one, shift_one, gain_two, shift_two = refs[:6]
    grad_qkv, bias_qkv, grad_out, grad_up, bias_up, grad_down, norms = refs[6:]
    here = place[1]
    rows = grad_up.shape[0]
    width = grad_out.shape[1] // members
    units = grad_up.shape[1] // members
    sums = [jnp.zeros((rows, 1), jnp.float32)] * 4
    for step in range(members):
        place_of = here ^ step
        message = first[step]
        line = message[rows : rows + 16, :].astype(jnp.float32)
        line = line[0:1, :units] + line[1:2, :units]
        values = message[:rows, :units].astype(jnp.float32)
        there = span(place_of, units)
        grad_up[:, there] = values * gain_two[...] + shift_two[...] * line
        bias_up[:, there] = line
        weight = w_up[:, there].astype(jnp.float32)
        sums[2] = sums[2] + jnp.sum(weight * values, axis=1, keepdims=True)
        sums[3] = sums[3] + jnp.sum(weight * line, axis=1, keepdims=True)
        grad_out[:, span(place_of, width)] = message[:rows, units : units + width].astype(
            jnp.float32
        )
        grad_down[:, there] = message[:rows, units + width :].astype(jnp.float32)
        message = second[step]
        whole_line = message[rows : rows + 16, :].astype(jnp.float32)
        for index in range(3):
            cut = slice(index * width, (index + 1) * width)
            line = whole_line[0:1, cut] + whole_line[1:2, cut]
            values = message[:rows, cut].astype(jnp.float32)
            there = span(place_of, width)
            grad_qkv[index, :, there] = values * gain_one[...] + shift_one[...] * line
            bias_qkv[index : index + 1, there] = line
            weight = w_qkv[:, index, there].astype(jnp.float32)
            sums[0] = sums[0] + jnp.sum(weight * values, axis=1, keepdims=True)
            sums[1] = sums[1] + jnp.sum(weight * line, axis=1, keepdims=True)
    lane = lax.broadcasted_iota(jnp.int32, (rows, 128), 1)
    result = jnp.zeros((rows, 128), jnp.float32)
    for index, total in enumerate(sums):
        result = jnp.where(lane == index, total, result)
    norms[...] = result


def sum_rows(kept, other):
    got = send(other, "tensor", 1)
    total = kept[0] + got[0].astype(jnp.float32)
    for step in range(1, kept.shape[0]):
        piece = (kept[step] + got[step].astype(jnp.float32)).astype(jnp.bfloat16)
        total = total + send(piece, "context", step).astype(jnp.float32)
    return total


def whole_sequences(
    tokens,
    cotangent,
    ln1_gain,
    ln1_bias,
    ln2_gain,
    ln2_bias,
    w_qkv,
    b_qkv,
    w_out,
    b_out,
    w_up,
    b_up,
    w_down,
    b_down,
):
    members, quarters = lax.axis_size("context"), lax.axis_size("fsdp")
    here, core = lax.axis_index("context"), lax.axis_index("tensor")
    rows, depth = tokens.shape
    half = rows // 2
    part = depth // quarters
    width = w_qkv.shape[2] // members
    units = w_up.shape[1] // members
    seq_len = rows * members
    low, wide = jnp.bfloat16, jnp.float32
    place = jnp.stack([lax.axis_index("fsdp"), here, core]).astype(jnp.int32)
    others = range(1, members)

    half_tokens, half_grad, own_first, own_second = call(
        pack_kernel,
        [
            ((half, depth), low),
            ((half, depth), low),
            ((part, 3 * width + units), low),
            ((part, width + units), low),
        ],
        place,
        tokens,
        cotangent,
        w_qkv,
        w_out,
        w_up,
        w_down,
    )
    seq_got = [send(half_tokens, "context", step) for step in others]
    seq_other = [send(values, "tensor", 1) for values in seq_got]
    first = [own_first] + [send(own_first, "fsdp", step) for step in range(1, quarters)]
    second = [own_second] + [send(own_second, "fsdp", step) for step in range(1, quarters)]
    grad_got = [send(half_grad, "context", step) for step in others]
    grad_other = [send(values, "tensor", 1) for values in grad_got]

    table = turn_tables(seq_len, width)
    line = lambda values: values.reshape(1, -1)
    hat, qkv, mixed, log_total, joined, slope, weights_one = call(
        lambda *refs: forward_kernel(members, quarters, *refs),
        [
            ((seq_len, depth), low),
            ((seq_len, 3 * width), low),
            ((seq_len, width), wide),
            ((seq_len, width), wide),
            ((seq_len, width + units), low),
            ((seq_len, units), wide),
            ((depth, 3 * width + units), low),
        ],
        place,
        tokens,
        *seq_got,
        *seq_other,
        *first,
        line(ln1_gain),
        line(ln1_bias),
        line(ln2_gain),
        line(ln2_bias),
        line(take(b_qkv, here * width, width, 1)),
        line(take(b_up, here * units, units)),
        table,
        scratch=[((seq_len, depth), low)],
    )
    weights_two, kept, other = call(
        lambda *refs: branch_kernel(members, *refs),
        [
            ((depth, width + units), low),
            ((members, half, depth), wide),
            ((members, half, depth), low),
        ],
        place,
        joined,
        *second,
    )
    branches = sum_rows(kept, other)
    own = take(tokens, core * half, half).astype(wide)
    result = both_halves((own + branches + b_out + b_down).astype(low))

    *messages, grad_heads, grad_up = call(
        lambda *refs: gradient_kernel(members, quarters, *refs),
        [((part + 16, width + 2 * units), low)] * quarters
        + [((seq_len, width), low), ((seq_len, units), low)],
        place,
        cotangent,
        *grad_got,
        *grad_other,
        hat,
        joined,
        slope,
        weights_two,
        scratch=[((seq_len, depth), low)],
    )
    early = messages[:1] + [send(messages[step], "fsdp", step) for step in range(1, quarters)]
    kept, other, *messages = call(
        lambda *refs: backward_kernel(members, quarters, *refs),
        [((members, half, depth), wide), ((members, half, depth), low)]
        + [((part + 16, 3 * width), low)] * quarters,
        place,
        qkv,
        mixed,
        log_total,
        grad_heads,
        grad_up,
        hat,
        weights_one,
        table,
        line(ln1_gain),
        line(ln2_gain),
        scratch=[
            ((seq_len, 3 * width), low),
            ((seq_len, width), wide),
            ((seq_len, width), wide),
        ],
    )
    late = messages[:1] + [send(messages[step], "fsdp", step) for step in range(1, quarters)]
    grad_norm = sum_rows(kept, other)

    lines = part // members

    def share(parts):
        total = parts[0].shape[1]
        *pieces, sums = call(
            lambda *refs: share_kernel(members, quarters, *refs),
            [((lines + 16, total), low)] * members + [((1, total), wide)],
            place,
            *parts,
        )
        return pieces[:1] + [send(pieces[step], "context", step) for step in others], sums

    early, sums = share(early)
    late, _ = share(late)

    center = own - jnp.mean(own, axis=-1, keepdims=True)
    factor = lax.rsqrt(jnp.mean(center * center, axis=-1, keepdims=True) + EPSILON)
    normed = center * factor
    grad_input = factor * (
        grad_norm
        - jnp.mean(grad_norm, axis=-1, keepdims=True)
        - normed * jnp.mean(grad_norm * normed, axis=-1, keepdims=True)
    )
    own_grad = take(cotangent, core * half, half).astype(wide)
    grad_tokens = both_halves(own_grad + grad_input)

    begin = lax.axis_index("fsdp") * part + here * lines
    column = lambda values: take(values, begin, lines).reshape(-1, 1)
    grad_w_qkv, bias_qkv, grad_w_out, grad_w_up, bias_up, grad_w_down, norms = call(
        lambda *refs: owner_kernel(members, *refs),
        [
            ((3, lines, members * width), wide),
            ((3, members * width), wide),
            ((lines, members * width), wide),
            ((lines, members * units), wide),
            ((1, members * units), wide),
            ((lines, members * units), wide),
            ((lines, 128), wide),
        ],
        place,
        *early,
        *late,
        take(w_qkv, here * lines, lines),
        take(w_up, here * lines, lines),
        column(ln1_gain),
        column(ln1_bias),
        column(ln2_gain),
        column(ln2_bias),
    )
    norms = norms[:, :4].T
    norms = norms + send(norms, "tensor", 1)
    columns = take(sums[0], here * lines, lines)
    return (
        result,
        grad_tokens,
        norms[0],
        norms[1],
        norms[2],
        norms[3],
        grad_w_qkv.transpose(1, 0, 2),
        bias_qkv,
        grad_w_out,
        columns,
        grad_w_up,
        bias_up[0],
        grad_w_down,
        columns,
    )


def power_of_two(number):
    return number & (number - 1) == 0


def on_device(*arrays):
    members = lax.axis_size("context")
    local_heads = arrays[6].shape[2] // HEAD
    units = arrays[10].shape[1]
    fits = (
        local_heads % members == 0
        and units % members == 0
        and lax.axis_size("tensor") == 2
        and power_of_two(members)
        and power_of_two(lax.axis_size("fsdp"))
    )
    return whole_sequences(*arrays) if fits else gathered_weights(*arrays)


def solution(mesh):
    in_specs = (
        P(("fsdp", "context"), None),
        P(("fsdp", "context"), None),
        P(),
        P(),
        P(),
        P(),
        P("fsdp", None, "tensor"),
        P(None, "tensor"),
        P("fsdp", "tensor"),
        P(),
        P("fsdp", "tensor"),
        P("tensor"),
        P("fsdp", "tensor"),
        P(),
    )
    out_specs = (
        P(("fsdp", "context"), None),
        P(("fsdp", "context"), None),
        P(("fsdp", "context")),
        P(("fsdp", "context")),
        P(("fsdp", "context")),
        P(("fsdp", "context")),
        P(("fsdp", "context"), None, "tensor"),
        P(None, "tensor"),
        P(("fsdp", "context"), "tensor"),
        P(("fsdp", "context")),
        P(("fsdp", "context"), "tensor"),
        P("tensor"),
        P(("fsdp", "context"), "tensor"),
        P(("fsdp", "context")),
    )
    return jax.shard_map(
        on_device, mesh=mesh, in_specs=in_specs, out_specs=out_specs, check_vma=False
    )
```

```python
import math

import jax
import jax.numpy as jnp
from jax import lax
from jax.experimental import pallas as pl
from jax.experimental.pallas import tpu as pltpu
from jax.sharding import PartitionSpec as P

HEAD = 64
ROT = 16


EPSILON = 1e-05
NEGATIVE = -1e30


def layer_norm(values, gain, shift):
    center = values - jnp.mean(values, axis=-1, keepdims=True)
    spread = jnp.mean(center * center, axis=-1, keepdims=True)
    return center * lax.rsqrt(spread + EPSILON) * gain + shift


def rotary_tables(positions, rot):
    half = rot // 2
    inverse = 1.0 / 10000.0 ** (jnp.arange(half, dtype=jnp.float32) * 2.0 / rot)
    angles = positions.astype(jnp.float32)[:, None] * inverse[None, :]
    return (jnp.cos(angles), jnp.sin(angles))


def rotate(values, cosine, sine):
    half = cosine.shape[-1]
    first = values[..., :half]
    second = values[..., half : 2 * half]
    cos_b = cosine[:, None, :]
    sin_b = sine[:, None, :]
    return jnp.concatenate(
        [first * cos_b - second * sin_b, second * cos_b + first * sin_b, values[..., 2 * half :]],
        axis=-1,
    )


def gelu_exact(values):
    return jax.nn.gelu(values, approximate=False)


def gathered_weights(
    tokens,
    cotangent,
    ln1_gain,
    ln1_bias,
    ln2_gain,
    ln2_bias,
    w_qkv,
    b_qkv,
    w_out,
    b_out,
    w_up,
    b_up,
    w_down,
    b_down,
):
    rows = tokens.shape[0]
    width = w_qkv.shape[2]
    local_heads = width // HEAD
    scale = 1.0 / math.sqrt(HEAD)
    seq_len = rows * lax.axis_size("context")
    whole = tokens.astype(jnp.float32)
    low_one = layer_norm(whole, ln1_gain, ln1_bias).astype(jnp.bfloat16)
    low_two = layer_norm(whole, ln2_gain, ln2_bias).astype(jnp.bfloat16)
    full_qkv, full_out, full_up, full_down = (
        lax.all_gather(w_qkv, "fsdp", axis=0, tiled=True),
        lax.all_gather(w_out, "fsdp", axis=0, tiled=True),
        lax.all_gather(w_up, "fsdp", axis=0, tiled=True),
        lax.all_gather(w_down, "fsdp", axis=0, tiled=True),
    )
    projected = (
        jnp.einsum("td,dke->tke", low_one, full_qkv, preferred_element_type=jnp.float32)
        + b_qkv[None]
    )
    positions = lax.axis_index("context") * rows + jnp.arange(rows, dtype=jnp.int32)
    last_query = positions[-1]
    cosine, sine = rotary_tables(positions, ROT)
    shaped = projected.reshape(rows, 3, local_heads, HEAD)
    query = rotate(shaped[:, 0], cosine, sine).astype(jnp.bfloat16)
    key = rotate(shaped[:, 1], cosine, sine).astype(jnp.bfloat16)
    value = shaped[:, 2].astype(jnp.bfloat16)
    pairs = jnp.stack([key.reshape(rows, width), value.reshape(rows, width)], axis=1)
    start_state = (
        jnp.full((local_heads, rows), NEGATIVE, jnp.float32),
        jnp.zeros((local_heads, rows), jnp.float32),
        jnp.zeros((local_heads, rows, HEAD), jnp.float32),
    )
    piece = lax.all_gather(pairs, "context", axis=0, tiled=True)
    size = piece.shape[0]
    block = math.gcd(size, math.lcm(512, rows))
    blocks = piece.reshape(size // block, block, 2, local_heads, HEAD)

    def forward_step(state, item):
        index, group = item
        first = index * block

        def forward_compute(inner):
            top, total, accum = inner
            key_pos = first + jnp.arange(block, dtype=jnp.int32)
            scores = (
                jnp.einsum("thd,rhd->htr", query, group[:, 0], preferred_element_type=jnp.float32)
                * scale
            )
            visible = key_pos[None, None, :] <= positions[None, :, None]
            scores = jnp.where(visible, scores, NEGATIVE)
            new_top = jnp.maximum(top, jnp.max(scores, axis=-1))
            weights = jnp.where(visible, jnp.exp(scores - new_top[..., None]), 0.0)
            factor = jnp.exp(top - new_top)
            total = total * factor + jnp.sum(weights, axis=-1)
            accum = accum * factor[..., None] + jnp.einsum(
                "htr,rhd->htd",
                weights.astype(jnp.bfloat16),
                group[:, 1],
                preferred_element_type=jnp.float32,
            )
            return (new_top, total, accum)

        return (lax.cond(first > last_query, lambda inner: inner, forward_compute, state), None)

    result, _ = lax.scan(
        forward_step, start_state, (jnp.arange(blocks.shape[0], dtype=jnp.int32), blocks)
    )
    top, total, accum = result
    attended = accum / total[..., None]
    log_total = top + jnp.log(total)
    mixed_low = attended.transpose(1, 0, 2).reshape(rows, width).astype(jnp.bfloat16)
    up_pre = jnp.dot(low_two, full_up, preferred_element_type=jnp.float32) + b_up
    active_low = gelu_exact(up_pre).astype(jnp.bfloat16)
    partial_sum = jnp.einsum(
        "te,de->td", mixed_low, full_out, preferred_element_type=jnp.float32
    ) + jnp.einsum("tf,df->td", active_low, full_down, preferred_element_type=jnp.float32)
    branches = lax.psum(partial_sum.astype(jnp.bfloat16), "tensor").astype(jnp.float32)
    result = (whole + branches + b_out + b_down).astype(jnp.bfloat16)
    grad_bias = jnp.sum(cotangent.astype(jnp.float32), axis=0)
    grad_w_out = jnp.einsum("td,te->de", cotangent, mixed_low, preferred_element_type=jnp.float32)
    grad_w_down = jnp.einsum("td,tf->df", cotangent, active_low, preferred_element_type=jnp.float32)
    grad_mixed = jnp.dot(cotangent, full_out, preferred_element_type=jnp.float32).astype(
        jnp.bfloat16
    )
    grad_active = jnp.dot(cotangent, full_down, preferred_element_type=jnp.float32)
    _, gelu_pull = jax.vjp(gelu_exact, up_pre)
    grad_up = gelu_pull(grad_active)[0].astype(jnp.bfloat16)
    grad_w_up = jnp.einsum("td,tf->df", low_two, grad_up, preferred_element_type=jnp.float32)
    grad_b_up = jnp.sum(grad_up.astype(jnp.float32), axis=0)
    grad_two = jnp.einsum("tf,df->td", grad_up, full_up, preferred_element_type=jnp.float32)
    grad_heads = grad_mixed.reshape(rows, local_heads, HEAD)
    delta = jnp.sum(grad_heads.astype(jnp.float32).transpose(1, 0, 2) * attended, axis=-1)
    query_start = jnp.zeros((local_heads, rows, HEAD), jnp.float32)
    back_state = (query_start, jnp.zeros((seq_len, 2, width), jnp.float32))
    piece = lax.all_gather(pairs, "context", axis=0, tiled=True)
    size = piece.shape[0]
    backward_block = math.gcd(size, math.lcm(512, rows))
    blocks = piece.reshape(size // backward_block, backward_block, 2, local_heads, HEAD)

    def backward_step(state, item):
        index, group = item
        first = index * backward_block

        def backward_compute(inner):
            grad_query = inner[0]
            key_pos = first + jnp.arange(backward_block, dtype=jnp.int32)
            scores = (
                jnp.einsum("thd,rhd->htr", query, group[:, 0], preferred_element_type=jnp.float32)
                * scale
            )
            visible = key_pos[None, None, :] <= positions[None, :, None]
            probs = jnp.where(visible, jnp.exp(scores - log_total[..., None]), 0.0)
            grad_probs = jnp.einsum(
                "thd,rhd->htr", grad_heads, group[:, 1], preferred_element_type=jnp.float32
            )
            grad_scores = (probs * (grad_probs - delta[..., None])).astype(jnp.bfloat16)
            grad_query = (
                grad_query
                + jnp.einsum(
                    "htr,rhd->htd", grad_scores, group[:, 0], preferred_element_type=jnp.float32
                )
                * scale
            )
            grad_value = jnp.einsum(
                "htr,thd->rhd",
                probs.astype(jnp.bfloat16),
                grad_heads,
                preferred_element_type=jnp.float32,
            )
            grad_key = (
                jnp.einsum("htr,thd->rhd", grad_scores, query, preferred_element_type=jnp.float32)
                * scale
            )
            update = jnp.stack(
                [
                    grad_key.reshape(backward_block, width),
                    grad_value.reshape(backward_block, width),
                ],
                axis=1,
            )
            return (grad_query, lax.dynamic_update_slice_in_dim(inner[1], update, first, 0))

        return (lax.cond(first > last_query, lambda inner: inner, backward_compute, state), None)

    result_state, _ = lax.scan(
        backward_step, back_state, (jnp.arange(blocks.shape[0], dtype=jnp.int32), blocks)
    )
    grad_query = result_state[0]
    grad_pairs = lax.psum_scatter(
        result_state[1].astype(jnp.bfloat16), "context", scatter_dimension=0, tiled=True
    ).astype(jnp.float32)
    _, turn_pull = jax.vjp(lambda values: rotate(values, cosine, sine), shaped[:, 0])
    grad_q_pre = turn_pull(grad_query.transpose(1, 0, 2))[0]
    grad_k_pre = turn_pull(grad_pairs[:, 0].reshape(rows, local_heads, HEAD))[0]
    grad_v_pre = grad_pairs[:, 1].reshape(rows, local_heads, HEAD)
    grad_proj = (
        jnp.stack([grad_q_pre, grad_k_pre, grad_v_pre], axis=1)
        .reshape(rows, 3, width)
        .astype(jnp.bfloat16)
    )
    grad_w_qkv = jnp.einsum("td,tke->dke", low_one, grad_proj, preferred_element_type=jnp.float32)
    grad_b_qkv = jnp.sum(grad_proj.astype(jnp.float32), axis=0)
    grad_one = jnp.einsum("tke,dke->td", grad_proj, full_qkv, preferred_element_type=jnp.float32)
    grad_one, grad_two = (
        lax.psum(grad_one.astype(jnp.bfloat16), "tensor").astype(jnp.float32),
        lax.psum(grad_two.astype(jnp.bfloat16), "tensor").astype(jnp.float32),
    )
    _, norm_pull_one = jax.vjp(layer_norm, whole, ln1_gain, ln1_bias)
    input_one, gain_one, shift_one = norm_pull_one(grad_one)
    _, norm_pull_two = jax.vjp(layer_norm, whole, ln2_gain, ln2_bias)
    input_two, gain_two, shift_two = norm_pull_two(grad_two)
    grad_tokens = cotangent.astype(jnp.float32) + input_one + input_two
    sum_qkv, sum_out, sum_up, sum_down, sum_g1, sum_c1, sum_g2, sum_c2, sum_bias = (
        lax.psum_scatter(grad_w_qkv, ("fsdp", "context"), scatter_dimension=0, tiled=True),
        lax.psum_scatter(grad_w_out, ("fsdp", "context"), scatter_dimension=0, tiled=True),
        lax.psum_scatter(grad_w_up, ("fsdp", "context"), scatter_dimension=0, tiled=True),
        lax.psum_scatter(grad_w_down, ("fsdp", "context"), scatter_dimension=0, tiled=True),
        lax.psum_scatter(gain_one, ("fsdp", "context"), scatter_dimension=0, tiled=True),
        lax.psum_scatter(shift_one, ("fsdp", "context"), scatter_dimension=0, tiled=True),
        lax.psum_scatter(gain_two, ("fsdp", "context"), scatter_dimension=0, tiled=True),
        lax.psum_scatter(shift_two, ("fsdp", "context"), scatter_dimension=0, tiled=True),
        lax.psum_scatter(grad_bias, ("fsdp", "context"), scatter_dimension=0, tiled=True),
    )
    bias_qkv, bias_up = lax.psum((grad_b_qkv, grad_b_up), ("fsdp", "context"))
    return (
        result,
        grad_tokens,
        sum_g1,
        sum_c1,
        sum_g2,
        sum_c2,
        sum_qkv,
        bias_qkv,
        sum_out,
        sum_bias,
        sum_up,
        bias_up,
        sum_down,
        sum_bias,
    )


MEBIBYTE = 1024 * 1024


def send(values, axis, step):
    size = lax.axis_size(axis)
    return lax.ppermute(values, axis, [(index, index ^ step) for index in range(size)])


def take(values, start, size, axis=0):
    return lax.dynamic_slice_in_dim(values, start, size, axis)


def both_halves(values):
    core = lax.axis_index("tensor")
    other = send(values, "tensor", 1)
    return jnp.concatenate(
        [jnp.where(core == 0, values, other), jnp.where(core == 0, other, values)], axis=0
    )


def call(body, outs, place, *arrays, scratch=(), after=(), flops=10**9, memory=16):
    skipped = len(after)

    def kernel(place_ref, *refs):
        body(place_ref, *refs[skipped:])

    return pl.pallas_call(
        kernel,
        out_shape=[jax.ShapeDtypeStruct(shape, kind) for shape, kind in outs],
        in_specs=[pl.BlockSpec(memory_space=pltpu.SMEM)]
        + [pl.BlockSpec(memory_space=pl.ANY)] * skipped
        + [pl.BlockSpec(memory_space=pltpu.VMEM)] * len(arrays),
        out_specs=[pl.BlockSpec(memory_space=pltpu.VMEM)] * len(outs),
        scratch_shapes=[pltpu.VMEM(shape, kind) for shape, kind in scratch],
        cost_estimate=pl.CostEstimate(flops=flops, bytes_accessed=0, transcendentals=0),
        compiler_params=pltpu.CompilerParams(vmem_limit_bytes=memory * MEBIBYTE),
    )(place, *after, *arrays)


def cut_call(body, outs, place, blocks, after=()):
    skipped = len(after)

    def kernel(place_ref, *refs):
        body(place_ref, *refs[skipped:])

    def whole(count):
        return lambda step, place_ref: (0,) * count

    return pl.pallas_call(
        kernel,
        grid_spec=pltpu.PrefetchScalarGridSpec(
            num_scalar_prefetch=1,
            grid=(1,),
            in_specs=[pl.BlockSpec(memory_space=pl.ANY)] * skipped
            + [
                pl.BlockSpec(shape, lambda step, place_ref, where=where: where(place_ref))
                for _, shape, where in blocks
            ],
            out_specs=[pl.BlockSpec(shape, whole(len(shape))) for shape, _ in outs],
        ),
        out_shape=[jax.ShapeDtypeStruct(shape, kind) for shape, kind in outs],
        compiler_params=pltpu.CompilerParams(vmem_limit_bytes=60 * MEBIBYTE),
    )(place, *after, *[array for array, _, _ in blocks])


def span(index, size, offset=0):
    return pl.ds(pl.multiple_of(index * size + offset, size), size)


def dot(first, second, contract=(1, 0)):
    return lax.dot_general(
        first, second, ((contract[:1], contract[1:]), ((), ())), preferred_element_type=jnp.float32
    )


def high_low(values):
    high = values.astype(jnp.bfloat16)
    return high, (values - high.astype(jnp.float32)).astype(jnp.bfloat16)


def small_rows(lines, width):
    rows = []
    for line in lines:
        rest = width - line.shape[1]
        if rest:
            line = jnp.concatenate([line, jnp.zeros((1, rest), jnp.float32)], axis=1)
        rows.extend(high_low(line))
    rows.append(jnp.zeros((16 - len(rows), width), jnp.bfloat16))
    return jnp.concatenate([row.astype(jnp.float32) for row in rows], axis=0).astype(jnp.bfloat16)


def turn(values, table, sign):
    wide = values.shape[1]
    half = ROT // 2
    ahead = pltpu.roll(values, wide - half, 1)
    behind = pltpu.roll(values, half, 1)
    return values * table[0] + sign * (ahead * table[1] + behind * table[2])


def turn_tables(seq_len, width):
    cosine, sine = rotary_tables(jnp.arange(seq_len, dtype=jnp.int32), ROT)
    rest = jnp.zeros((seq_len, HEAD - ROT), jnp.float32)
    none = jnp.zeros_like(sine)
    one = jnp.concatenate([cosine, cosine, rest + 1.0], axis=1)
    ahead = jnp.concatenate([-sine, none, rest], axis=1)
    behind = jnp.concatenate([none, sine, rest], axis=1)
    heads = width // HEAD
    return jnp.stack([jnp.tile(part, (1, heads)) for part in (one, ahead, behind)])


def pack_kernel(
    place, tokens, cotangent, qkv, up, out, down, qkv_rows, up_rows, first, second, weights, own_qkv, own_up
):
    width, units = qkv.shape[2], up.shape[1]
    first[...] = tokens[...]
    second[...] = cotangent[...]
    for part in range(3):
        weights[:, part * width : (part + 1) * width] = qkv[part]
    cut = 3 * width + units
    weights[:, 3 * width : cut] = up[...]
    weights[:, cut : cut + width] = out[...]
    weights[:, cut + width :] = down[...]
    own_qkv[...] = qkv_rows[...]
    own_up[...] = up_rows[...]


def assemble_rows(place, whole, own, got, other):
    here, core = place[1], place[2]
    rows, half = own.shape[0], own.shape[0] // 2
    whole[span(here, rows), :] = own[...]
    for step in range(1, len(got) + 1):
        start = (here ^ step) * rows
        mine = pl.ds(pl.multiple_of(start + core * half, half), half)
        whole[mine, :] = got[step - 1][...]
        twins = pl.ds(pl.multiple_of(start + (1 - core) * half, half), half)
        whole[twins, :] = other[step - 1][...]


def assemble_width(place, whole, parts, columns):
    rows = parts[0].shape[0]
    for step, part in enumerate(parts):
        whole[span(place[0] ^ step, rows), :] = part[:, columns]


def column_sums(values):
    return dot(jnp.ones((16, values.shape[0]), jnp.bfloat16), values)[0:1, :]


def head_mask(width, head):
    lane = lax.broadcasted_iota(jnp.int32, (1, width), 1)
    return (lane >= head * HEAD) & (lane < (head + 1) * HEAD)


def only_head(values, head):
    return jnp.where(head_mask(values.shape[1], head), values, jnp.zeros_like(values))


def causal(rows, first, keys):
    row = lax.broadcasted_iota(jnp.int32, (rows, keys), 0) + first
    return lax.broadcasted_iota(jnp.int32, (rows, keys), 1) <= row


def forward_kernel(members, quarters, place, *refs):
    own, refs = refs[0], refs[1:]
    got, refs = refs[: members - 1], refs[members - 1 :]
    other, refs = refs[: members - 1], refs[members - 1 :]
    parts, refs = refs[:quarters], refs[quarters:]
    gain_one, shift_one, gain_two, shift_two, bias_qkv, bias_up, table = refs[:7]
    hat_turned, qkv, mixed, log_total, joined, slope, weights, weights_two = refs[7:15]
    seq, low_one, low_two = refs[15:]
    assemble_rows(place, seq, own, got, other)
    cut = weights.shape[1]
    assemble_width(place, weights, parts, slice(0, cut))
    assemble_width(place, weights_two, parts, slice(cut, cut + weights_two.shape[1]))
    seq_len = seq.shape[0]
    width = mixed.shape[1]
    block = own.shape[0]
    for start in range(0, seq_len, block):
        rows = slice(start, start + block)
        values = seq[rows, :].astype(jnp.float32)
        center = values - jnp.mean(values, axis=-1, keepdims=True)
        spread = jnp.mean(center * center, axis=-1, keepdims=True)
        normed = center * lax.rsqrt(spread + EPSILON)
        hat_turned[:, rows] = normed.astype(jnp.bfloat16).T
        low_one[rows, :] = (normed * gain_one[...] + shift_one[...]).astype(jnp.bfloat16)
        low_two[rows, :] = (normed * gain_two[...] + shift_two[...]).astype(jnp.bfloat16)
    turning = [table[part] for part in range(3)]
    query = dot(low_one[...], weights[:, :width]) + bias_qkv[:, :width]
    query = turn(query, turning, 1.0).astype(jnp.bfloat16)
    qkv[:, :width] = query * (1.0 / math.sqrt(HEAD))
    key = dot(low_one[...], weights[:, width : 2 * width]) + bias_qkv[:, width : 2 * width]
    qkv[:, width : 2 * width] = turn(key, turning, 1.0).astype(jnp.bfloat16)
    value = dot(low_one[...], weights[:, 2 * width : 3 * width]) + bias_qkv[:, 2 * width :]
    qkv[:, 2 * width :] = value.astype(jnp.bfloat16)
    pre = dot(low_two[...], weights[:, 3 * width :]) + bias_up[...]
    phi = 0.5 * (1.0 + lax.erf(pre * (1.0 / math.sqrt(2.0))))
    density = jnp.exp(-0.5 * pre * pre) * (1.0 / math.sqrt(2.0 * math.pi))
    joined[:, width:] = (pre * phi).astype(jnp.bfloat16)
    slope[...] = phi + pre * density
    for start in range(0, seq_len, block):
        rows = slice(start, start + block)
        keys = start + block
        visible = causal(block, start, keys)
        result = jnp.zeros((block, width), jnp.float32)
        logs = jnp.zeros((block, width), jnp.float32)
        for head in range(width // HEAD):
            scores = dot(only_head(qkv[rows, :width], head), qkv[:keys, width : 2 * width], (1, 1))
            scores = jnp.where(visible, scores, NEGATIVE)
            top = jnp.max(scores, axis=-1, keepdims=True)
            expo = jnp.exp(scores - top)
            total = jnp.sum(expo, axis=-1, keepdims=True)
            attended = dot(expo.astype(jnp.bfloat16), qkv[:keys, 2 * width :]) / total
            mask = head_mask(width, head)
            result = jnp.where(mask, attended, result)
            logs = jnp.where(mask, top + jnp.log(total), logs)
        mixed[rows, :] = result
        log_total[rows, :] = logs
        joined[rows, :width] = result.astype(jnp.bfloat16)


def gather_halves(place, values, mine, twins):
    here, core = place[1], place[2]
    members, half = mine.shape[:2]
    for step in range(members):
        start = (here ^ step) * (2 * half)
        mine[step] = values[pl.ds(pl.multiple_of(start + core * half, half), half), :]
        twins[step] = values[pl.ds(pl.multiple_of(start + (1 - core) * half, half), half), :]


def flat(values):
    return values.reshape(values.shape[0] * values.shape[1], values.shape[2])


def branch_kernel(place, joined, weights, kept, other, mine, twins):
    gather_halves(place, joined, mine, twins)
    kept[...] = dot(flat(mine[...]), weights[...], (1, 1)).reshape(kept.shape)
    partial = dot(flat(twins[...]), weights[...], (1, 1))
    other[...] = partial.astype(jnp.bfloat16).reshape(other.shape)


def gradient_kernel(members, quarters, place, own, *refs):
    got, refs = refs[: members - 1], refs[members - 1 :]
    other, refs = refs[: members - 1], refs[members - 1 :]
    hat_turned, joined, slope, weights = refs[:4]
    messages, refs = refs[4 : 4 + quarters], refs[4 + quarters :]
    grad_heads, grad_up, grad, partial = refs
    assemble_rows(place, grad, own, got, other)
    depth = grad.shape[1]
    width = grad_heads.shape[1]
    units = grad_up.shape[1]
    grad_heads[...] = dot(grad[...], weights[:, :width]).astype(jnp.bfloat16)
    grad_up[...] = (dot(grad[...], weights[:, width:]) * slope[...]).astype(jnp.bfloat16)
    partial[:, :units] = dot(hat_turned[...], grad_up[...]).astype(jnp.bfloat16)
    partial[:, units:] = dot(grad[...], joined[...], (0, 0)).astype(jnp.bfloat16)
    biases = column_sums(grad_up[...])
    part = depth // quarters
    for step in range(quarters):
        quarter = span(place[0] ^ step, part)
        message = messages[step]
        message[:part, :] = partial[quarter, :]
        sums = column_sums(grad[:, quarter])
        message[part:, :] = small_rows([biases, sums], message.shape[1])


def backward_kernel(block, place, *refs):
    qkv, mixed, log_total, grad_heads, table, grad_proj, sum_key, sum_value = refs
    seq_len, width = mixed.shape
    scale = 1.0 / math.sqrt(HEAD)
    sum_key[...] = jnp.zeros_like(sum_key)
    sum_value[...] = jnp.zeros_like(sum_value)
    for start in range(0, seq_len, block):
        rows = slice(start, start + block)
        keys = start + block
        visible = causal(block, start, keys)
        key, value = qkv[:keys, width : 2 * width], qkv[:keys, 2 * width :]
        grad_query = jnp.zeros((block, width), jnp.float32)
        grad_key = jnp.zeros((keys, width), jnp.float32)
        grad_value = jnp.zeros((keys, width), jnp.float32)
        product = grad_heads[rows, :].astype(jnp.float32) * mixed[rows, :]
        for head in range(width // HEAD):
            query = only_head(qkv[rows, :width], head)
            heads = only_head(grad_heads[rows, :], head)
            delta = jnp.sum(only_head(product, head), axis=-1, keepdims=True)
            logs = log_total[rows, head * HEAD : head * HEAD + 1]
            scores = dot(query, key, (1, 1))
            probs = jnp.where(visible, jnp.exp(scores - logs), 0.0)
            grad_scores = (probs * (dot(heads, value, (1, 1)) - delta)).astype(jnp.bfloat16)
            grad_query = jnp.where(
                head_mask(width, head), dot(grad_scores, key) * scale, grad_query
            )
            grad_key = grad_key + dot(grad_scores, query, (0, 0))
            grad_value = grad_value + dot(probs.astype(jnp.bfloat16), heads, (0, 0))
        turning = [table[part, rows, :] for part in range(3)]
        grad_proj[rows, :width] = turn(grad_query, turning, -1.0).astype(jnp.bfloat16)
        sum_key[:keys, :] += grad_key
        sum_value[:keys, :] += grad_value
    turning = [table[part] for part in range(3)]
    grad_proj[:, width : 2 * width] = turn(sum_key[...], turning, -1.0).astype(jnp.bfloat16)
    grad_proj[:, 2 * width :] = sum_value[...].astype(jnp.bfloat16)


def norm_gradient_kernel(quarters, place, *refs):
    grad_proj, grad_up, hat_turned, weights, gain_one, gain_two, kept, other = refs[:8]
    messages, refs = refs[8 : 8 + quarters], refs[8 + quarters :]
    mine_proj, twins_proj, mine_up, twins_up, weight_sum = refs
    cut = grad_proj.shape[1]
    gather_halves(place, grad_proj, mine_proj, twins_proj)
    gather_halves(place, grad_up, mine_up, twins_up)

    def gradient(proj, up):
        first = dot(flat(proj[...]), weights[:, :cut], (1, 1)) * gain_one[...]
        return first + dot(flat(up[...]), weights[:, cut:], (1, 1)) * gain_two[...]

    other[...] = gradient(twins_proj, twins_up).astype(jnp.bfloat16).reshape(other.shape)
    kept[...] = gradient(mine_proj, mine_up).reshape(kept.shape)
    weight_sum[...] = dot(hat_turned[...], grad_proj[...]).astype(jnp.bfloat16)
    part = hat_turned.shape[0] // quarters
    biases = column_sums(grad_proj[...])
    for step in range(quarters):
        message = messages[step]
        message[:part, :] = weight_sum[span(place[0] ^ step, part), :]
        message[part:, :] = small_rows([biases], message.shape[1])


def add_parts(parts, chosen):
    total = parts[0][chosen, :].astype(jnp.float32)
    for part in parts[1:]:
        total = total + part[chosen, :].astype(jnp.float32)
    return total


def share_early_kernel(members, quarters, place, *refs):
    parts, pieces, line = refs[:quarters], refs[quarters:-1], refs[-1]
    rows = pieces[0].shape[0] - 16
    for step in range(members):
        chosen = span(place[1] ^ step, rows)
        pieces[step][:rows, :] = add_parts(parts, chosen).astype(jnp.bfloat16)
    total = add_parts(parts, slice(rows * members, rows * members + 16))
    line[...] = total[2:3] + total[3:4]
    small = small_rows([total[0:1] + total[1:2]], total.shape[1])
    for step in range(members):
        pieces[step][rows:, :] = small


def share_late_kernel(members, quarters, place, *refs):
    parts, refs = refs[:quarters], refs[quarters:]
    early, pieces = refs[:members], refs[members:]
    rows = pieces[0].shape[0] - 16
    width = early[0].shape[1]
    for step in range(members):
        chosen = span(place[1] ^ step, rows)
        pieces[step][:, :width] = early[step][...]
        pieces[step][:rows, width:] = add_parts(parts, chosen).astype(jnp.bfloat16)
    total = add_parts(parts, slice(rows * members, rows * members + 16))
    small = small_rows([total[0:1] + total[1:2]], total.shape[1])
    for step in range(members):
        pieces[step][rows:, width:] = small


def owner_kernel(members, place, *refs):
    pieces, refs = refs[:members], refs[members:]
    w_qkv, w_up, lines = refs[:3]
    grad_qkv, bias_qkv, grad_out, grad_up, bias_up, grad_down, norms = refs[3:]
    gain_one, shift_one, gain_two, shift_two = [lines[:, i : i + 1] for i in range(4)]
    here = place[1]
    rows = grad_up.shape[0]
    width = grad_out.shape[1] // members
    units = grad_up.shape[1] // members
    sums = [jnp.zeros((rows, 1), jnp.float32)] * 4
    for step in range(members):
        place_of = here ^ step
        message = pieces[step]
        line = message[rows : rows + 16, :].astype(jnp.float32)
        line = line[0:1, :units] + line[1:2, :units]
        values = message[:rows, :units].astype(jnp.float32)
        there = span(place_of, units)
        grad_up[:, there] = values * gain_two + shift_two * line
        bias_up[:, there] = line
        weight = w_up[:, there].astype(jnp.float32)
        sums[2] = sums[2] + jnp.sum(weight * values, axis=1, keepdims=True)
        sums[3] = sums[3] + jnp.sum(weight * line, axis=1, keepdims=True)
        grad_out[:, span(place_of, width)] = message[:rows, units : units + width].astype(
            jnp.float32
        )
        begin = 2 * units + width
        grad_down[:, there] = message[:rows, units + width : begin].astype(jnp.float32)
        whole_line = message[rows : rows + 16, :].astype(jnp.float32)
        for index in range(3):
            cut = slice(begin + index * width, begin + (index + 1) * width)
            line = whole_line[0:1, cut] + whole_line[1:2, cut]
            values = message[:rows, cut].astype(jnp.float32)
            there = span(place_of, width)
            grad_qkv[index, :, there] = values * gain_one + shift_one * line
            bias_qkv[index : index + 1, there] = line
            weight = w_qkv[index, :, there].astype(jnp.float32)
            sums[0] = sums[0] + jnp.sum(weight * values, axis=1, keepdims=True)
            sums[1] = sums[1] + jnp.sum(weight * line, axis=1, keepdims=True)
    lane = lax.broadcasted_iota(jnp.int32, (rows, 128), 1)
    result = jnp.zeros((rows, 128), jnp.float32)
    for index, total in enumerate(sums):
        result = jnp.where(lane == index, total, result)
    norms[...] = result


def halve_kernel(place, kept, got, stay, leave):
    for index in range(stay.shape[0]):
        stay[index] = kept[2 * index] + got[2 * index].astype(jnp.float32)
        odd = kept[2 * index + 1] + got[2 * index + 1].astype(jnp.float32)
        leave[index] = odd.astype(jnp.bfloat16)


def first_halving(place, kept, other, after=()):
    members, half, depth = kept.shape
    return call(
        halve_kernel,
        [((members // 2, half, depth), jnp.float32), ((members // 2, half, depth), jnp.bfloat16)],
        place,
        kept,
        send(other, "tensor", 1),
        after=after,
        flops=1,
    )


def last_halvings(total):
    step = 1
    while total.shape[0] > 1:
        step = 2 * step
        leave = send(total[1::2].astype(jnp.bfloat16), "context", step)
        total = total[0::2] + leave.astype(jnp.float32)
    return total[0]


def gather(values, axis):
    parts = [values]
    for step in range(1, lax.axis_size(axis)):
        top = 1 << (step.bit_length() - 1)
        low = step ^ top
        parts.append(send(values, axis, step) if not low else send(parts[top], axis, low))
    return parts


def gather_halves_apart(values):
    if lax.axis_size("fsdp") != 4:
        return gather(values, "fsdp")
    half = values.shape[0] // 2
    one, two = send(values, "fsdp", 1), send(values, "fsdp", 2)
    three = [send(one[:half], "fsdp", 2), send(two[half:], "fsdp", 1)]
    return [values, one, two, jnp.concatenate(three)]


def whole_sequences(
    tokens,
    cotangent,
    ln1_gain,
    ln1_bias,
    ln2_gain,
    ln2_bias,
    w_qkv,
    b_qkv,
    w_out,
    b_out,
    w_up,
    b_up,
    w_down,
    b_down,
):
    members, quarters = lax.axis_size("context"), lax.axis_size("fsdp")
    here, core = lax.axis_index("context"), lax.axis_index("tensor")
    rows, depth = tokens.shape
    half = rows // 2
    part = depth // quarters
    lines = part // members
    width = w_qkv.shape[2] // members
    units = w_up.shape[1] // members
    seq_len = rows * members
    low, wide = jnp.bfloat16, jnp.float32
    place = jnp.stack([lax.axis_index("fsdp"), here, core]).astype(jnp.int32)
    others = range(1, members)
    parted_qkv = w_qkv.transpose(1, 0, 2)

    cuts = 4 * width + 2 * units
    half_tokens, half_grad, own_weights, qkv_rows, up_rows = cut_call(
        pack_kernel,
        [
            ((half, depth), low),
            ((half, depth), low),
            ((part, cuts), low),
            ((3, lines, members * width), low),
            ((lines, members * units), low),
        ],
        place,
        [
            (tokens, (half, depth), lambda at: (at[2], 0)),
            (cotangent, (half, depth), lambda at: (at[2], 0)),
            (parted_qkv, (3, part, width), lambda at: (0, 0, at[1])),
            (w_up, (part, units), lambda at: (0, at[1])),
            (w_out, (part, width), lambda at: (0, at[1])),
            (w_down, (part, units), lambda at: (0, at[1])),
            (parted_qkv, (3, lines, members * width), lambda at: (0, at[1], 0)),
            (w_up, (lines, members * units), lambda at: (at[1], 0)),
        ],
    )
    seq_got = gather(half_tokens, "context")[1:]
    seq_other = [send(values, "tensor", 1) for values in seq_got]
    grad_got = gather(half_grad, "context")[1:]
    grad_other = [send(values, "tensor", 1) for values in grad_got]
    parts = gather_halves_apart(own_weights)

    table = turn_tables(seq_len, width)
    line = lambda values: values.reshape(1, -1)
    hat_turned, qkv, mixed, log_total, joined, slope, weights_one, weights_two = call(
        lambda *refs: forward_kernel(members, quarters, *refs),
        [
            ((depth, seq_len), low),
            ((seq_len, 3 * width), low),
            ((seq_len, width), wide),
            ((seq_len, width), wide),
            ((seq_len, width + units), low),
            ((seq_len, units), wide),
            ((depth, 3 * width + units), low),
            ((depth, width + units), low),
        ],
        place,
        tokens,
        *seq_got,
        *seq_other,
        *parts,
        line(ln1_gain),
        line(ln1_bias),
        line(ln2_gain),
        line(ln2_bias),
        line(take(b_qkv, here * width, width, 1)),
        line(take(b_up, here * units, units)),
        table,
        scratch=[((seq_len, depth), low)] * 3,
        flops=12 * 10**9,
        memory=60,
    )
    kept, other = call(
        branch_kernel,
        [((members, half, depth), wide), ((members, half, depth), low)],
        place,
        joined,
        weights_two,
        scratch=[((members, half, width + units), low)] * 2,
        flops=4 * 10**9,
        memory=60,
    )
    *messages, grad_heads, grad_up = call(
        lambda *refs: gradient_kernel(members, quarters, *refs),
        [((part + 16, width + 2 * units), low)] * quarters
        + [((seq_len, width), low), ((seq_len, units), low)],
        place,
        cotangent,
        *grad_got,
        *grad_other,
        hat_turned,
        joined,
        slope,
        weights_two,
        scratch=[
            ((seq_len, depth), low),
            ((depth, width + 2 * units), low),
        ],
        after=[other],
        flops=11 * 10**9,
        memory=60,
    )
    early = messages[:1] + [send(messages[step], "fsdp", step) for step in range(1, quarters)]
    stay, leave = first_halving(place, kept, other, after=[grad_heads])
    leave = send(leave, "context", 1)
    (grad_proj,) = call(
        lambda *refs: backward_kernel(rows, *refs),
        [((seq_len, 3 * width), low)],
        place,
        qkv,
        mixed,
        log_total,
        grad_heads,
        table,
        scratch=[((seq_len, width), wide)] * 2,
        after=[stay],
        flops=1,
        memory=60,
    )
    total = stay + leave.astype(wide)
    kept, other, *messages = call(
        lambda *refs: norm_gradient_kernel(quarters, *refs),
        [((members, half, depth), wide), ((members, half, depth), low)]
        + [((part + 16, 3 * width), low)] * quarters,
        place,
        grad_proj,
        grad_up,
        hat_turned,
        weights_one,
        line(ln1_gain),
        line(ln2_gain),
        scratch=[((members, half, 3 * width), low)] * 2
        + [((members, half, units), low)] * 2
        + [((depth, 3 * width), low)],
        after=[total],
        flops=1,
        memory=60,
    )
    late = messages[:1] + [send(messages[step], "fsdp", step) for step in range(1, quarters)]

    branches = last_halvings(total)
    *early, sums = call(
        lambda *refs: share_early_kernel(members, quarters, *refs),
        [((lines + 16, width + 2 * units), low)] * members + [((1, width + 2 * units), wide)],
        place,
        *early,
        flops=20 * 10**9,
    )
    stay, leave = first_halving(place, kept, other, after=[sums, branches, *late[1:]])
    leave = send(leave, "context", 1)
    pieces = call(
        lambda *refs: share_late_kernel(members, quarters, *refs),
        [((lines + 16, 4 * width + 2 * units), low)] * members,
        place,
        *late,
        *early,
        after=[stay],
        flops=3 * 10**9,
    )
    pieces = [pieces[0]] + [send(pieces[step], "context", step) for step in others]

    own = take(tokens, core * half, half).astype(wide)
    result = both_halves((own + branches + b_out + b_down).astype(low))
    grad_norm = last_halvings(stay + leave.astype(wide))
    center = own - jnp.mean(own, axis=-1, keepdims=True)
    factor = lax.rsqrt(jnp.mean(center * center, axis=-1, keepdims=True) + EPSILON)
    normed = center * factor
    grad_input = factor * (
        grad_norm
        - jnp.mean(grad_norm, axis=-1, keepdims=True)
        - normed * jnp.mean(grad_norm * normed, axis=-1, keepdims=True)
    )
    own_grad = take(cotangent, core * half, half).astype(wide)
    grad_half = own_grad + grad_input
    grad_tokens = both_halves(grad_half)

    begin = lax.axis_index("fsdp") * part + here * lines
    columns = jnp.stack([ln1_gain, ln1_bias, ln2_gain, ln2_bias])
    grad_w_qkv, bias_qkv, grad_w_out, grad_w_up, bias_up, grad_w_down, norms = call(
        lambda *refs: owner_kernel(members, *refs),
        [
            ((3, lines, members * width), wide),
            ((3, members * width), wide),
            ((lines, members * width), wide),
            ((lines, members * units), wide),
            ((1, members * units), wide),
            ((lines, members * units), wide),
            ((lines, 128), wide),
        ],
        place,
        *pieces,
        qkv_rows,
        up_rows,
        take(columns, begin, lines, 1).T,
        after=[leave],
    )
    norms = norms[:, :4].T
    norms = norms + send(norms, "tensor", 1)
    columns = take(sums[0], here * lines, lines)
    return (
        result,
        grad_tokens,
        norms[0],
        norms[1],
        norms[2],
        norms[3],
        grad_w_qkv.transpose(1, 0, 2),
        bias_qkv,
        grad_w_out,
        columns,
        grad_w_up,
        bias_up[0],
        grad_w_down,
        columns,
    )


def power_of_two(number):
    return number & (number - 1) == 0


def on_device(*arrays):
    members = lax.axis_size("context")
    local_heads = arrays[6].shape[2] // HEAD
    units = arrays[10].shape[1]
    fits = (
        members > 1
        and local_heads % members == 0
        and units % members == 0
        and lax.axis_size("tensor") == 2
        and power_of_two(members)
        and power_of_two(lax.axis_size("fsdp"))
    )
    return whole_sequences(*arrays) if fits else gathered_weights(*arrays)


def solution(mesh):
    in_specs = (
        P(("fsdp", "context"), None),
        P(("fsdp", "context"), None),
        P(),
        P(),
        P(),
        P(),
        P("fsdp", None, "tensor"),
        P(None, "tensor"),
        P("fsdp", "tensor"),
        P(),
        P("fsdp", "tensor"),
        P("tensor"),
        P("fsdp", "tensor"),
        P(),
    )
    out_specs = (
        P(("fsdp", "context"), None),
        P(("fsdp", "context"), None),
        P(("fsdp", "context")),
        P(("fsdp", "context")),
        P(("fsdp", "context")),
        P(("fsdp", "context")),
        P(("fsdp", "context"), None, "tensor"),
        P(None, "tensor"),
        P(("fsdp", "context"), "tensor"),
        P(("fsdp", "context")),
        P(("fsdp", "context"), "tensor"),
        P("tensor"),
        P(("fsdp", "context"), "tensor"),
        P(("fsdp", "context")),
    )
    return jax.shard_map(
        on_device, mesh=mesh, in_specs=in_specs, out_specs=out_specs, check_vma=False
    )
```

```python
import math

import jax
import jax.numpy as jnp
from jax import lax
from jax.experimental import pallas as pl
from jax.experimental.pallas import tpu as pltpu
from jax.sharding import PartitionSpec as P

HEAD = 64
ROT = 16


EPSILON = 1e-05
NEGATIVE = -1e30


def layer_norm(values, gain, shift):
    center = values - jnp.mean(values, axis=-1, keepdims=True)
    spread = jnp.mean(center * center, axis=-1, keepdims=True)
    return center * lax.rsqrt(spread + EPSILON) * gain + shift


def rotary_tables(positions, rot):
    half = rot // 2
    inverse = 1.0 / 10000.0 ** (jnp.arange(half, dtype=jnp.float32) * 2.0 / rot)
    angles = positions.astype(jnp.float32)[:, None] * inverse[None, :]
    return (jnp.cos(angles), jnp.sin(angles))


def rotate(values, cosine, sine):
    half = cosine.shape[-1]
    first = values[..., :half]
    second = values[..., half : 2 * half]
    cos_b = cosine[:, None, :]
    sin_b = sine[:, None, :]
    return jnp.concatenate(
        [first * cos_b - second * sin_b, second * cos_b + first * sin_b, values[..., 2 * half :]],
        axis=-1,
    )


def gelu_exact(values):
    return jax.nn.gelu(values, approximate=False)


def gathered_weights(
    tokens,
    cotangent,
    ln1_gain,
    ln1_bias,
    ln2_gain,
    ln2_bias,
    w_qkv,
    b_qkv,
    w_out,
    b_out,
    w_up,
    b_up,
    w_down,
    b_down,
):
    rows = tokens.shape[0]
    width = w_qkv.shape[2]
    local_heads = width // HEAD
    scale = 1.0 / math.sqrt(HEAD)
    seq_len = rows * lax.axis_size("context")
    whole = tokens.astype(jnp.float32)
    low_one = layer_norm(whole, ln1_gain, ln1_bias).astype(jnp.bfloat16)
    low_two = layer_norm(whole, ln2_gain, ln2_bias).astype(jnp.bfloat16)
    full_qkv, full_out, full_up, full_down = (
        lax.all_gather(w_qkv, "fsdp", axis=0, tiled=True),
        lax.all_gather(w_out, "fsdp", axis=0, tiled=True),
        lax.all_gather(w_up, "fsdp", axis=0, tiled=True),
        lax.all_gather(w_down, "fsdp", axis=0, tiled=True),
    )
    projected = (
        jnp.einsum("td,dke->tke", low_one, full_qkv, preferred_element_type=jnp.float32)
        + b_qkv[None]
    )
    positions = lax.axis_index("context") * rows + jnp.arange(rows, dtype=jnp.int32)
    last_query = positions[-1]
    cosine, sine = rotary_tables(positions, ROT)
    shaped = projected.reshape(rows, 3, local_heads, HEAD)
    query = rotate(shaped[:, 0], cosine, sine).astype(jnp.bfloat16)
    key = rotate(shaped[:, 1], cosine, sine).astype(jnp.bfloat16)
    value = shaped[:, 2].astype(jnp.bfloat16)
    pairs = jnp.stack([key.reshape(rows, width), value.reshape(rows, width)], axis=1)
    start_state = (
        jnp.full((local_heads, rows), NEGATIVE, jnp.float32),
        jnp.zeros((local_heads, rows), jnp.float32),
        jnp.zeros((local_heads, rows, HEAD), jnp.float32),
    )
    piece = lax.all_gather(pairs, "context", axis=0, tiled=True)
    size = piece.shape[0]
    block = math.gcd(size, math.lcm(512, rows))
    blocks = piece.reshape(size // block, block, 2, local_heads, HEAD)

    def forward_step(state, item):
        index, group = item
        first = index * block

        def forward_compute(inner):
            top, total, accum = inner
            key_pos = first + jnp.arange(block, dtype=jnp.int32)
            scores = (
                jnp.einsum("thd,rhd->htr", query, group[:, 0], preferred_element_type=jnp.float32)
                * scale
            )
            visible = key_pos[None, None, :] <= positions[None, :, None]
            scores = jnp.where(visible, scores, NEGATIVE)
            new_top = jnp.maximum(top, jnp.max(scores, axis=-1))
            weights = jnp.where(visible, jnp.exp(scores - new_top[..., None]), 0.0)
            factor = jnp.exp(top - new_top)
            total = total * factor + jnp.sum(weights, axis=-1)
            accum = accum * factor[..., None] + jnp.einsum(
                "htr,rhd->htd",
                weights.astype(jnp.bfloat16),
                group[:, 1],
                preferred_element_type=jnp.float32,
            )
            return (new_top, total, accum)

        return (lax.cond(first > last_query, lambda inner: inner, forward_compute, state), None)

    result, _ = lax.scan(
        forward_step, start_state, (jnp.arange(blocks.shape[0], dtype=jnp.int32), blocks)
    )
    top, total, accum = result
    attended = accum / total[..., None]
    log_total = top + jnp.log(total)
    mixed_low = attended.transpose(1, 0, 2).reshape(rows, width).astype(jnp.bfloat16)
    up_pre = jnp.dot(low_two, full_up, preferred_element_type=jnp.float32) + b_up
    active_low = gelu_exact(up_pre).astype(jnp.bfloat16)
    partial_sum = jnp.einsum(
        "te,de->td", mixed_low, full_out, preferred_element_type=jnp.float32
    ) + jnp.einsum("tf,df->td", active_low, full_down, preferred_element_type=jnp.float32)
    branches = lax.psum(partial_sum.astype(jnp.bfloat16), "tensor").astype(jnp.float32)
    result = (whole + branches + b_out + b_down).astype(jnp.bfloat16)
    grad_bias = jnp.sum(cotangent.astype(jnp.float32), axis=0)
    grad_w_out = jnp.einsum("td,te->de", cotangent, mixed_low, preferred_element_type=jnp.float32)
    grad_w_down = jnp.einsum("td,tf->df", cotangent, active_low, preferred_element_type=jnp.float32)
    grad_mixed = jnp.dot(cotangent, full_out, preferred_element_type=jnp.float32).astype(
        jnp.bfloat16
    )
    grad_active = jnp.dot(cotangent, full_down, preferred_element_type=jnp.float32)
    _, gelu_pull = jax.vjp(gelu_exact, up_pre)
    grad_up = gelu_pull(grad_active)[0].astype(jnp.bfloat16)
    grad_w_up = jnp.einsum("td,tf->df", low_two, grad_up, preferred_element_type=jnp.float32)
    grad_b_up = jnp.sum(grad_up.astype(jnp.float32), axis=0)
    grad_two = jnp.einsum("tf,df->td", grad_up, full_up, preferred_element_type=jnp.float32)
    grad_heads = grad_mixed.reshape(rows, local_heads, HEAD)
    delta = jnp.sum(grad_heads.astype(jnp.float32).transpose(1, 0, 2) * attended, axis=-1)
    query_start = jnp.zeros((local_heads, rows, HEAD), jnp.float32)
    back_state = (query_start, jnp.zeros((seq_len, 2, width), jnp.float32))
    piece = lax.all_gather(pairs, "context", axis=0, tiled=True)
    size = piece.shape[0]
    backward_block = math.gcd(size, math.lcm(512, rows))
    blocks = piece.reshape(size // backward_block, backward_block, 2, local_heads, HEAD)

    def backward_step(state, item):
        index, group = item
        first = index * backward_block

        def backward_compute(inner):
            grad_query = inner[0]
            key_pos = first + jnp.arange(backward_block, dtype=jnp.int32)
            scores = (
                jnp.einsum("thd,rhd->htr", query, group[:, 0], preferred_element_type=jnp.float32)
                * scale
            )
            visible = key_pos[None, None, :] <= positions[None, :, None]
            probs = jnp.where(visible, jnp.exp(scores - log_total[..., None]), 0.0)
            grad_probs = jnp.einsum(
                "thd,rhd->htr", grad_heads, group[:, 1], preferred_element_type=jnp.float32
            )
            grad_scores = (probs * (grad_probs - delta[..., None])).astype(jnp.bfloat16)
            grad_query = (
                grad_query
                + jnp.einsum(
                    "htr,rhd->htd", grad_scores, group[:, 0], preferred_element_type=jnp.float32
                )
                * scale
            )
            grad_value = jnp.einsum(
                "htr,thd->rhd",
                probs.astype(jnp.bfloat16),
                grad_heads,
                preferred_element_type=jnp.float32,
            )
            grad_key = (
                jnp.einsum("htr,thd->rhd", grad_scores, query, preferred_element_type=jnp.float32)
                * scale
            )
            update = jnp.stack(
                [
                    grad_key.reshape(backward_block, width),
                    grad_value.reshape(backward_block, width),
                ],
                axis=1,
            )
            return (grad_query, lax.dynamic_update_slice_in_dim(inner[1], update, first, 0))

        return (lax.cond(first > last_query, lambda inner: inner, backward_compute, state), None)

    result_state, _ = lax.scan(
        backward_step, back_state, (jnp.arange(blocks.shape[0], dtype=jnp.int32), blocks)
    )
    grad_query = result_state[0]
    grad_pairs = lax.psum_scatter(
        result_state[1].astype(jnp.bfloat16), "context", scatter_dimension=0, tiled=True
    ).astype(jnp.float32)
    _, turn_pull = jax.vjp(lambda values: rotate(values, cosine, sine), shaped[:, 0])
    grad_q_pre = turn_pull(grad_query.transpose(1, 0, 2))[0]
    grad_k_pre = turn_pull(grad_pairs[:, 0].reshape(rows, local_heads, HEAD))[0]
    grad_v_pre = grad_pairs[:, 1].reshape(rows, local_heads, HEAD)
    grad_proj = (
        jnp.stack([grad_q_pre, grad_k_pre, grad_v_pre], axis=1)
        .reshape(rows, 3, width)
        .astype(jnp.bfloat16)
    )
    grad_w_qkv = jnp.einsum("td,tke->dke", low_one, grad_proj, preferred_element_type=jnp.float32)
    grad_b_qkv = jnp.sum(grad_proj.astype(jnp.float32), axis=0)
    grad_one = jnp.einsum("tke,dke->td", grad_proj, full_qkv, preferred_element_type=jnp.float32)
    grad_one, grad_two = (
        lax.psum(grad_one.astype(jnp.bfloat16), "tensor").astype(jnp.float32),
        lax.psum(grad_two.astype(jnp.bfloat16), "tensor").astype(jnp.float32),
    )
    _, norm_pull_one = jax.vjp(layer_norm, whole, ln1_gain, ln1_bias)
    input_one, gain_one, shift_one = norm_pull_one(grad_one)
    _, norm_pull_two = jax.vjp(layer_norm, whole, ln2_gain, ln2_bias)
    input_two, gain_two, shift_two = norm_pull_two(grad_two)
    grad_tokens = cotangent.astype(jnp.float32) + input_one + input_two
    sum_qkv, sum_out, sum_up, sum_down, sum_g1, sum_c1, sum_g2, sum_c2, sum_bias = (
        lax.psum_scatter(grad_w_qkv, ("fsdp", "context"), scatter_dimension=0, tiled=True),
        lax.psum_scatter(grad_w_out, ("fsdp", "context"), scatter_dimension=0, tiled=True),
        lax.psum_scatter(grad_w_up, ("fsdp", "context"), scatter_dimension=0, tiled=True),
        lax.psum_scatter(grad_w_down, ("fsdp", "context"), scatter_dimension=0, tiled=True),
        lax.psum_scatter(gain_one, ("fsdp", "context"), scatter_dimension=0, tiled=True),
        lax.psum_scatter(shift_one, ("fsdp", "context"), scatter_dimension=0, tiled=True),
        lax.psum_scatter(gain_two, ("fsdp", "context"), scatter_dimension=0, tiled=True),
        lax.psum_scatter(shift_two, ("fsdp", "context"), scatter_dimension=0, tiled=True),
        lax.psum_scatter(grad_bias, ("fsdp", "context"), scatter_dimension=0, tiled=True),
    )
    bias_qkv, bias_up = lax.psum((grad_b_qkv, grad_b_up), ("fsdp", "context"))
    return (
        result,
        grad_tokens,
        sum_g1,
        sum_c1,
        sum_g2,
        sum_c2,
        sum_qkv,
        bias_qkv,
        sum_out,
        sum_bias,
        sum_up,
        bias_up,
        sum_down,
        sum_bias,
    )


MEBIBYTE = 1024 * 1024


def send(values, axis, step):
    size = lax.axis_size(axis)
    return lax.ppermute(values, axis, [(index, index ^ step) for index in range(size)])


def take(values, start, size, axis=0):
    return lax.dynamic_slice_in_dim(values, start, size, axis)


def both_halves(values):
    core = lax.axis_index("tensor")
    other = send(values, "tensor", 1)
    return jnp.concatenate(
        [jnp.where(core == 0, values, other), jnp.where(core == 0, other, values)], axis=0
    )


def call(body, outs, place, *arrays, scratch=(), after=(), far=(), copies=0, flops=10**9, memory=16):
    skipped = len(after)
    anywhere = pl.BlockSpec(memory_space=pl.ANY)
    near = pl.BlockSpec(memory_space=pltpu.VMEM)

    def kernel(place_ref, *refs):
        body(place_ref, *refs[skipped:])

    scratch_shapes = [pltpu.VMEM(shape, kind) for shape, kind in scratch]
    if copies:
        scratch_shapes.append(pltpu.SemaphoreType.DMA((copies,)))
    return pl.pallas_call(
        kernel,
        out_shape=[jax.ShapeDtypeStruct(shape, kind) for shape, kind in outs],
        in_specs=[pl.BlockSpec(memory_space=pltpu.SMEM)]
        + [anywhere] * (skipped + len(far))
        + [near] * len(arrays),
        out_specs=[anywhere if copies else near] * len(outs),
        scratch_shapes=scratch_shapes,
        cost_estimate=pl.CostEstimate(flops=flops, bytes_accessed=0, transcendentals=0),
        compiler_params=pltpu.CompilerParams(vmem_limit_bytes=memory * MEBIBYTE),
    )(place, *after, *far, *arrays)


class Copies:
    def __init__(self, semaphores):
        self.semaphores, self.all = semaphores, []

    def start(self, source, target):
        copy = pltpu.make_async_copy(source, target, self.semaphores.at[len(self.all)])
        copy.start()
        self.all.append(copy)
        return copy


def wait(copies):
    for copy in copies:
        copy.wait()


def cut_call(body, outs, place, blocks, after=()):
    skipped = len(after)

    def kernel(place_ref, *refs):
        body(place_ref, *refs[skipped:])

    def whole(count):
        return lambda step, place_ref: (0,) * count

    return pl.pallas_call(
        kernel,
        grid_spec=pltpu.PrefetchScalarGridSpec(
            num_scalar_prefetch=1,
            grid=(1,),
            in_specs=[pl.BlockSpec(memory_space=pl.ANY)] * skipped
            + [
                pl.BlockSpec(shape, lambda step, place_ref, where=where: where(place_ref))
                for _, shape, where in blocks
            ],
            out_specs=[pl.BlockSpec(shape, whole(len(shape))) for shape, _ in outs],
        ),
        out_shape=[jax.ShapeDtypeStruct(shape, kind) for shape, kind in outs],
        compiler_params=pltpu.CompilerParams(vmem_limit_bytes=60 * MEBIBYTE),
    )(place, *after, *[array for array, _, _ in blocks])


def span(index, size, offset=0):
    return pl.ds(pl.multiple_of(index * size + offset, size), size)


def dot(first, second, contract=(1, 0)):
    return lax.dot_general(
        first, second, ((contract[:1], contract[1:]), ((), ())), preferred_element_type=jnp.float32
    )


def high_low(values):
    high = values.astype(jnp.bfloat16)
    return high, (values - high.astype(jnp.float32)).astype(jnp.bfloat16)


def small_rows(lines, width):
    rows = []
    for line in lines:
        rest = width - line.shape[1]
        if rest:
            line = jnp.concatenate([line, jnp.zeros((1, rest), jnp.float32)], axis=1)
        rows.extend(high_low(line))
    rows.append(jnp.zeros((16 - len(rows), width), jnp.bfloat16))
    return jnp.concatenate([row.astype(jnp.float32) for row in rows], axis=0).astype(jnp.bfloat16)


def turn(values, table, sign):
    wide = values.shape[1]
    half = ROT // 2
    ahead = pltpu.roll(values, wide - half, 1)
    behind = pltpu.roll(values, half, 1)
    return values * table[0] + sign * (ahead * table[1] + behind * table[2])


def turn_tables(seq_len, width):
    cosine, sine = rotary_tables(jnp.arange(seq_len, dtype=jnp.int32), ROT)
    rest = jnp.zeros((seq_len, HEAD - ROT), jnp.float32)
    none = jnp.zeros_like(sine)
    one = jnp.concatenate([cosine, cosine, rest + 1.0], axis=1)
    ahead = jnp.concatenate([-sine, none, rest], axis=1)
    behind = jnp.concatenate([none, sine, rest], axis=1)
    heads = width // HEAD
    return jnp.stack([jnp.tile(part, (1, heads)) for part in (one, ahead, behind)])


def pack_kernel(
    place, tokens, cotangent, qkv, up, out, down, qkv_rows, up_rows, first, second, weights, own_qkv, own_up
):
    width, units = qkv.shape[2], up.shape[1]
    first[...] = tokens[...]
    second[...] = cotangent[...]
    for part in range(3):
        weights[:, part * width : (part + 1) * width] = qkv[part]
    cut = 3 * width + units
    weights[:, 3 * width : cut] = up[...]
    weights[:, cut : cut + width] = out[...]
    weights[:, cut + width :] = down[...]
    own_qkv[...] = qkv_rows[...]
    own_up[...] = up_rows[...]


def assemble_rows(place, copies, whole, own, got, other):
    here, core = place[1], place[2]
    rows, half = own.shape[0], own.shape[0] // 2
    started = [copies.start(own, whole.at[span(here, rows)])]
    for step in range(1, len(got) + 1):
        start = (here ^ step) * rows
        mine = pl.ds(pl.multiple_of(start + core * half, half), half)
        twins = pl.ds(pl.multiple_of(start + (1 - core) * half, half), half)
        started.append(copies.start(got[step - 1], whole.at[mine]))
        started.append(copies.start(other[step - 1], whole.at[twins]))
    return started


def assemble_width(place, copies, whole, parts):
    rows, columns = parts[0].shape[0], whole.shape[1]
    return [
        copies.start(part.at[:, pl.ds(0, columns)], whole.at[span(place[0] ^ step, rows)])
        for step, part in enumerate(parts)
    ]


def column_sums(values):
    return dot(jnp.ones((16, values.shape[0]), jnp.bfloat16), values)[0:1, :]


def head_mask(width, head):
    lane = lax.broadcasted_iota(jnp.int32, (1, width), 1)
    return (lane >= head * HEAD) & (lane < (head + 1) * HEAD)


def only_head(values, head):
    return jnp.where(head_mask(values.shape[1], head), values, jnp.zeros_like(values))


def causal(rows, first, keys):
    row = lax.broadcasted_iota(jnp.int32, (rows, keys), 0) + first
    return lax.broadcasted_iota(jnp.int32, (rows, keys), 1) <= row


def gather_halves(place, values, mine, twins):
    here, core = place[1], place[2]
    members, half = mine.shape[:2]
    for step in range(members):
        start = (here ^ step) * (2 * half)
        mine[step] = values[pl.ds(pl.multiple_of(start + core * half, half), half), :]
        twins[step] = values[pl.ds(pl.multiple_of(start + (1 - core) * half, half), half), :]


def flat(values):
    return values.reshape(values.shape[0] * values.shape[1], values.shape[2])


def send_parts(place, copies, sums, small, messages):
    part = sums.shape[0] // len(messages)
    started = []
    for step, message in enumerate(messages):
        chosen = sums.at[span(place[0] ^ step, part)]
        started.append(copies.start(chosen, message.at[pl.ds(0, part)]))
        rows = pl.ds(part, small.shape[1])
        started.append(copies.start(small.at[step], message.at[rows]))
    return started


def first_kernel(members, quarters, place, *refs):
    refs = list(refs)

    def some(count):
        taken = refs[:count]
        del refs[:count]
        return taken

    rows_of = [some(1) + [some(members - 1), some(members - 1)] for _ in range(2)]
    parts = some(quarters)
    (table_far,) = some(1)
    gain_one, shift_one, gain_two, shift_two, bias_qkv, bias_up = some(6)
    hat_out, qkv_out, mixed_out, log_out, heads_out, up_out, kept_out, other_out = some(8)
    messages = some(quarters)
    seq, grad, weights, table, low_one, low_two, hat, qkv, mixed, log_total = some(10)
    joined, slope, grad_heads, grad_up, kept, other, mine, twins, sums_w, small = some(10)
    copies = Copies(refs[0])
    row_copies = assemble_rows(place, copies, seq, *rows_of[0])
    weight_copies = assemble_width(place, copies, weights, parts)
    weight_copies.append(copies.start(table_far, table))
    grad_copies = assemble_rows(place, copies, grad, *rows_of[1])
    block = seq.shape[0] // members
    seq_len = seq.shape[0]
    width = mixed.shape[1]
    cut = 3 * width + slope.shape[1]
    wait(row_copies)
    for start in range(0, seq_len, block):
        rows = slice(start, start + block)
        values = seq[rows, :].astype(jnp.float32)
        center = values - jnp.mean(values, axis=-1, keepdims=True)
        spread = jnp.mean(center * center, axis=-1, keepdims=True)
        normed = center * lax.rsqrt(spread + EPSILON)
        hat[:, rows] = normed.astype(jnp.bfloat16).T
        low_one[rows, :] = (normed * gain_one[...] + shift_one[...]).astype(jnp.bfloat16)
        low_two[rows, :] = (normed * gain_two[...] + shift_two[...]).astype(jnp.bfloat16)
    leaving = [copies.start(hat, hat_out)]
    wait(weight_copies)
    turning = [table[part] for part in range(3)]
    query = dot(low_one[...], weights[:, :width]) + bias_qkv[:, :width]
    query = turn(query, turning, 1.0).astype(jnp.bfloat16)
    qkv[:, :width] = query * (1.0 / math.sqrt(HEAD))
    key = dot(low_one[...], weights[:, width : 2 * width]) + bias_qkv[:, width : 2 * width]
    qkv[:, width : 2 * width] = turn(key, turning, 1.0).astype(jnp.bfloat16)
    value = dot(low_one[...], weights[:, 2 * width : 3 * width]) + bias_qkv[:, 2 * width :]
    qkv[:, 2 * width :] = value.astype(jnp.bfloat16)
    leaving.append(copies.start(qkv, qkv_out))
    pre = dot(low_two[...], weights[:, 3 * width : cut]) + bias_up[...]
    phi = 0.5 * (1.0 + lax.erf(pre * (1.0 / math.sqrt(2.0))))
    density = jnp.exp(-0.5 * pre * pre) * (1.0 / math.sqrt(2.0 * math.pi))
    joined[:, width:] = (pre * phi).astype(jnp.bfloat16)
    slope[...] = phi + pre * density
    for start in range(0, seq_len, block):
        rows = slice(start, start + block)
        keys = start + block
        visible = causal(block, start, keys)
        result = jnp.zeros((block, width), jnp.float32)
        logs = jnp.zeros((block, width), jnp.float32)
        for head in range(width // HEAD):
            scores = dot(only_head(qkv[rows, :width], head), qkv[:keys, width : 2 * width], (1, 1))
            scores = jnp.where(visible, scores, NEGATIVE)
            top = jnp.max(scores, axis=-1, keepdims=True)
            expo = jnp.exp(scores - top)
            total = jnp.sum(expo, axis=-1, keepdims=True)
            attended = dot(expo.astype(jnp.bfloat16), qkv[:keys, 2 * width :]) / total
            mask = head_mask(width, head)
            result = jnp.where(mask, attended, result)
            logs = jnp.where(mask, top + jnp.log(total), logs)
        mixed[rows, :] = result
        log_total[rows, :] = logs
        joined[rows, :width] = result.astype(jnp.bfloat16)
    leaving += [copies.start(mixed, mixed_out), copies.start(log_total, log_out)]
    gather_halves(place, joined, mine, twins)
    partial = dot(flat(twins[...]), weights[:, cut:], (1, 1))
    other[...] = partial.astype(jnp.bfloat16).reshape(other.shape)
    leaving.append(copies.start(other, other_out))
    kept[...] = dot(flat(mine[...]), weights[:, cut:], (1, 1)).reshape(kept.shape)
    leaving.append(copies.start(kept, kept_out))
    wait(grad_copies)
    back = cut + width
    grad_heads[...] = dot(grad[...], weights[:, cut:back]).astype(jnp.bfloat16)
    leaving.append(copies.start(grad_heads, heads_out))
    grad_up[...] = (dot(grad[...], weights[:, back:]) * slope[...]).astype(jnp.bfloat16)
    leaving.append(copies.start(grad_up, up_out))
    units = grad_up.shape[1]
    sums_w[:, :units] = dot(hat[...], grad_up[...]).astype(jnp.bfloat16)
    sums_w[:, units:] = dot(grad[...], joined[...], (0, 0)).astype(jnp.bfloat16)
    biases = column_sums(grad_up[...])
    part = grad.shape[1] // quarters
    for step in range(quarters):
        sums = column_sums(grad[:, span(place[0] ^ step, part)])
        small[step] = small_rows([biases, sums], small.shape[2])
    wait(leaving + send_parts(place, copies, sums_w, small, messages))


def pair_kernel(place, kept, got, own, *pieces):
    own[...] = kept[0] + got[0].astype(jnp.float32)
    for step, piece in enumerate(pieces, 1):
        piece[...] = (kept[step] + got[step].astype(jnp.float32)).astype(jnp.bfloat16)


def halve_kernel(place, kept, got, stay, leave):
    for index in range(stay.shape[0]):
        stay[index] = kept[2 * index] + got[2 * index].astype(jnp.float32)
        odd = kept[2 * index + 1] + got[2 * index + 1].astype(jnp.float32)
        leave[index] = odd.astype(jnp.bfloat16)


def second_kernel(block, quarters, place, *refs):
    qkv_far, mixed_far, log_far, heads_far, table_far, up_far, hat_far = refs[:7]
    parts, refs = refs[7 : 7 + quarters], refs[7 + quarters :]
    gain_one, gain_two, kept_out, other_out = refs[:4]
    messages, refs = refs[4 : 4 + quarters], refs[4 + quarters :]
    qkv, mixed, log_total, grad_heads, table, grad_up, hat, weights = refs[:8]
    grad_proj, sum_key, sum_value, kept, other = refs[8:13]
    mine_proj, twins_proj, mine_up, twins_up, sums_w, small, semaphores = refs[13:]
    copies = Copies(semaphores)
    far = (qkv_far, mixed_far, log_far, heads_far, table_far)
    near = (qkv, mixed, log_total, grad_heads, table)
    first_copies = [copies.start(source, target) for source, target in zip(far, near)]
    later_copies = [copies.start(up_far, grad_up), copies.start(hat_far, hat)]
    later_copies += assemble_width(place, copies, weights, parts)
    seq_len, width = mixed.shape
    scale = 1.0 / math.sqrt(HEAD)
    wait(first_copies)
    sum_key[...] = jnp.zeros_like(sum_key)
    sum_value[...] = jnp.zeros_like(sum_value)
    for start in range(0, seq_len, block):
        rows = slice(start, start + block)
        keys = start + block
        visible = causal(block, start, keys)
        key, value = qkv[:keys, width : 2 * width], qkv[:keys, 2 * width :]
        grad_query = jnp.zeros((block, width), jnp.float32)
        grad_key = jnp.zeros((keys, width), jnp.float32)
        grad_value = jnp.zeros((keys, width), jnp.float32)
        product = grad_heads[rows, :].astype(jnp.float32) * mixed[rows, :]
        for head in range(width // HEAD):
            query = only_head(qkv[rows, :width], head)
            heads = only_head(grad_heads[rows, :], head)
            delta = jnp.sum(only_head(product, head), axis=-1, keepdims=True)
            logs = log_total[rows, head * HEAD : head * HEAD + 1]
            scores = dot(query, key, (1, 1))
            probs = jnp.where(visible, jnp.exp(scores - logs), 0.0)
            grad_scores = (probs * (dot(heads, value, (1, 1)) - delta)).astype(jnp.bfloat16)
            grad_query = jnp.where(
                head_mask(width, head), dot(grad_scores, key) * scale, grad_query
            )
            grad_key = grad_key + dot(grad_scores, query, (0, 0))
            grad_value = grad_value + dot(probs.astype(jnp.bfloat16), heads, (0, 0))
        turning = [table[part, rows, :] for part in range(3)]
        grad_proj[rows, :width] = turn(grad_query, turning, -1.0).astype(jnp.bfloat16)
        sum_key[:keys, :] += grad_key
        sum_value[:keys, :] += grad_value
    turning = [table[part] for part in range(3)]
    grad_proj[:, width : 2 * width] = turn(sum_key[...], turning, -1.0).astype(jnp.bfloat16)
    grad_proj[:, 2 * width :] = sum_value[...].astype(jnp.bfloat16)
    wait(later_copies)
    cut = grad_proj.shape[1]
    gather_halves(place, grad_proj, mine_proj, twins_proj)
    gather_halves(place, grad_up, mine_up, twins_up)

    def gradient(proj, up):
        first = dot(flat(proj[...]), weights[:, :cut], (1, 1)) * gain_one[...]
        return first + dot(flat(up[...]), weights[:, cut:], (1, 1)) * gain_two[...]

    other[...] = gradient(twins_proj, twins_up).astype(jnp.bfloat16).reshape(other.shape)
    leaving = [copies.start(other, other_out)]
    kept[...] = gradient(mine_proj, mine_up).reshape(kept.shape)
    leaving.append(copies.start(kept, kept_out))
    sums_w[...] = dot(hat[...], grad_proj[...]).astype(jnp.bfloat16)
    lines = small_rows([column_sums(grad_proj[...])], small.shape[2])
    for step in range(quarters):
        small[step] = lines
    wait(leaving + send_parts(place, copies, sums_w, small, messages))


def add_parts(parts, chosen):
    total = parts[0][chosen, :].astype(jnp.float32)
    for part in parts[1:]:
        total = total + part[chosen, :].astype(jnp.float32)
    return total


def share_early_kernel(members, quarters, place, *refs):
    parts, pieces, line = refs[:quarters], refs[quarters:-1], refs[-1]
    rows = pieces[0].shape[0] - 16
    for step in range(members):
        chosen = span(place[1] ^ step, rows)
        pieces[step][:rows, :] = add_parts(parts, chosen).astype(jnp.bfloat16)
    total = add_parts(parts, slice(rows * members, rows * members + 16))
    line[...] = total[2:3] + total[3:4]
    small = small_rows([total[0:1] + total[1:2]], total.shape[1])
    for step in range(members):
        pieces[step][rows:, :] = small


def share_late_kernel(members, quarters, place, *refs):
    parts, refs = refs[:quarters], refs[quarters:]
    early, pieces = refs[:members], refs[members:]
    rows = pieces[0].shape[0] - 16
    width = early[0].shape[1]
    for step in range(members):
        chosen = span(place[1] ^ step, rows)
        pieces[step][:, :width] = early[step][...]
        pieces[step][:rows, width:] = add_parts(parts, chosen).astype(jnp.bfloat16)
    total = add_parts(parts, slice(rows * members, rows * members + 16))
    small = small_rows([total[0:1] + total[1:2]], total.shape[1])
    for step in range(members):
        pieces[step][rows:, width:] = small


def owner_kernel(members, place, *refs):
    pieces, refs = refs[:members], refs[members:]
    w_qkv, w_up, lines = refs[:3]
    grad_qkv, bias_qkv, grad_out, grad_up, bias_up, grad_down, norms = refs[3:]
    gain_one, shift_one, gain_two, shift_two = [lines[:, i : i + 1] for i in range(4)]
    here = place[1]
    rows = grad_up.shape[0]
    width = grad_out.shape[1] // members
    units = grad_up.shape[1] // members
    sums = [jnp.zeros((rows, 1), jnp.float32)] * 4
    for step in range(members):
        place_of = here ^ step
        message = pieces[step]
        line = message[rows : rows + 16, :].astype(jnp.float32)
        line = line[0:1, :units] + line[1:2, :units]
        values = message[:rows, :units].astype(jnp.float32)
        there = span(place_of, units)
        grad_up[:, there] = values * gain_two + shift_two * line
        bias_up[:, there] = line
        weight = w_up[:, there].astype(jnp.float32)
        sums[2] = sums[2] + jnp.sum(weight * values, axis=1, keepdims=True)
        sums[3] = sums[3] + jnp.sum(weight * line, axis=1, keepdims=True)
        grad_out[:, span(place_of, width)] = message[:rows, units : units + width].astype(
            jnp.float32
        )
        begin = 2 * units + width
        grad_down[:, there] = message[:rows, units + width : begin].astype(jnp.float32)
        whole_line = message[rows : rows + 16, :].astype(jnp.float32)
        for index in range(3):
            cut = slice(begin + index * width, begin + (index + 1) * width)
            line = whole_line[0:1, cut] + whole_line[1:2, cut]
            values = message[:rows, cut].astype(jnp.float32)
            there = span(place_of, width)
            grad_qkv[index, :, there] = values * gain_one + shift_one * line
            bias_qkv[index : index + 1, there] = line
            weight = w_qkv[index, :, there].astype(jnp.float32)
            sums[0] = sums[0] + jnp.sum(weight * values, axis=1, keepdims=True)
            sums[1] = sums[1] + jnp.sum(weight * line, axis=1, keepdims=True)
    lane = lax.broadcasted_iota(jnp.int32, (rows, 128), 1)
    result = jnp.zeros((rows, 128), jnp.float32)
    for index, total in enumerate(sums):
        result = jnp.where(lane == index, total, result)
    norms[...] = result


def pair_kernel(place, kept, got, own, *pieces):
    own[...] = kept[0] + got[0].astype(jnp.float32)
    for step, piece in enumerate(pieces, 1):
        piece[...] = (kept[step] + got[step].astype(jnp.float32)).astype(jnp.bfloat16)


def halve_kernel(place, kept, got, stay, leave):
    for index in range(stay.shape[0]):
        stay[index] = kept[2 * index] + got[2 * index].astype(jnp.float32)
        odd = kept[2 * index + 1] + got[2 * index + 1].astype(jnp.float32)
        leave[index] = odd.astype(jnp.bfloat16)


def first_halving(place, kept, other, after=()):
    members, half, depth = kept.shape
    return call(
        halve_kernel,
        [((members // 2, half, depth), jnp.float32), ((members // 2, half, depth), jnp.bfloat16)],
        place,
        kept,
        send(other, "tensor", 1),
        after=after,
        flops=1,
    )


def last_halvings(total):
    step = 1
    while total.shape[0] > 1:
        step = 2 * step
        leave = send(total[1::2].astype(jnp.bfloat16), "context", step)
        total = total[0::2] + leave.astype(jnp.float32)
    return total[0]


def gather(values, axis):
    parts = [values]
    for step in range(1, lax.axis_size(axis)):
        top = 1 << (step.bit_length() - 1)
        low = step ^ top
        parts.append(send(values, axis, step) if not low else send(parts[top], axis, low))
    return parts


def gather_halves_apart(values):
    if lax.axis_size("fsdp") != 4:
        return gather(values, "fsdp")
    half = values.shape[0] // 2
    one, two = send(values, "fsdp", 1), send(values, "fsdp", 2)
    three = [send(one[:half], "fsdp", 2), send(two[half:], "fsdp", 1)]
    return [values, one, two, jnp.concatenate(three)]


def whole_sequences(
    tokens,
    cotangent,
    ln1_gain,
    ln1_bias,
    ln2_gain,
    ln2_bias,
    w_qkv,
    b_qkv,
    w_out,
    b_out,
    w_up,
    b_up,
    w_down,
    b_down,
):
    members, quarters = lax.axis_size("context"), lax.axis_size("fsdp")
    here, core = lax.axis_index("context"), lax.axis_index("tensor")
    rows, depth = tokens.shape
    half = rows // 2
    part = depth // quarters
    lines = part // members
    width = w_qkv.shape[2] // members
    units = w_up.shape[1] // members
    seq_len = rows * members
    low, wide = jnp.bfloat16, jnp.float32
    place = jnp.stack([lax.axis_index("fsdp"), here, core]).astype(jnp.int32)
    others = range(1, members)
    parted_qkv = w_qkv.transpose(1, 0, 2)

    cuts = 4 * width + 2 * units
    half_tokens, half_grad, own_weights, qkv_rows, up_rows = cut_call(
        pack_kernel,
        [
            ((half, depth), low),
            ((half, depth), low),
            ((part, cuts), low),
            ((3, lines, members * width), low),
            ((lines, members * units), low),
        ],
        place,
        [
            (tokens, (half, depth), lambda at: (at[2], 0)),
            (cotangent, (half, depth), lambda at: (at[2], 0)),
            (parted_qkv, (3, part, width), lambda at: (0, 0, at[1])),
            (w_up, (part, units), lambda at: (0, at[1])),
            (w_out, (part, width), lambda at: (0, at[1])),
            (w_down, (part, units), lambda at: (0, at[1])),
            (parted_qkv, (3, lines, members * width), lambda at: (0, at[1], 0)),
            (w_up, (lines, members * units), lambda at: (at[1], 0)),
        ],
    )
    seq_got = gather(half_tokens, "context")[1:]
    seq_other = [send(values, "tensor", 1) for values in seq_got]
    grad_got = gather(half_grad, "context")[1:]
    grad_other = [send(values, "tensor", 1) for values in grad_got]
    parts = gather_halves_apart(own_weights)

    table = turn_tables(seq_len, width)
    line = lambda values: values.reshape(1, -1)
    hat, qkv, mixed, log_total, grad_heads, grad_up, kept, other, *messages = call(
        lambda *refs: first_kernel(members, quarters, *refs),
        [
            ((depth, seq_len), low),
            ((seq_len, 3 * width), low),
            ((seq_len, width), wide),
            ((seq_len, width), wide),
            ((seq_len, width), low),
            ((seq_len, units), low),
            ((members, half, depth), wide),
            ((members, half, depth), low),
        ]
        + [((part + 16, width + 2 * units), low)] * quarters,
        place,
        line(ln1_gain),
        line(ln1_bias),
        line(ln2_gain),
        line(ln2_bias),
        line(take(b_qkv, here * width, width, 1)),
        line(take(b_up, here * units, units)),
        far=[tokens, *seq_got, *seq_other, cotangent, *grad_got, *grad_other, *parts, table],
        scratch=[
            ((seq_len, depth), low),
            ((seq_len, depth), low),
            ((depth, cuts), low),
            ((3, seq_len, width), wide),
            ((seq_len, depth), low),
            ((seq_len, depth), low),
            ((depth, seq_len), low),
            ((seq_len, 3 * width), low),
            ((seq_len, width), wide),
            ((seq_len, width), wide),
            ((seq_len, width + units), low),
            ((seq_len, units), wide),
            ((seq_len, width), low),
            ((seq_len, units), low),
            ((members, half, depth), wide),
            ((members, half, depth), low),
            ((members, half, width + units), low),
            ((members, half, width + units), low),
            ((depth, width + 2 * units), low),
            ((quarters, 16, width + 2 * units), low),
        ],
        copies=2 * (2 * members - 1) + quarters + 1 + 8 + 2 * quarters,
        flops=25 * 10**9,
        memory=60,
    )
    early = messages[:1] + [send(messages[step], "fsdp", step) for step in range(1, quarters)]
    branches, *pieces = call(
        pair_kernel,
        [((half, depth), wide)] + [((half, depth), low)] * (members - 1),
        place,
        kept,
        send(other, "tensor", 1),
        flops=1,
    )
    branch_pieces = [send(pieces[step - 1], "context", step) for step in others]
    kept, other, *messages = call(
        lambda *refs: second_kernel(rows, quarters, *refs),
        [((members, half, depth), wide), ((members, half, depth), low)]
        + [((part + 16, 3 * width), low)] * quarters,
        place,
        line(ln1_gain),
        line(ln2_gain),
        far=[qkv, mixed, log_total, grad_heads, table, grad_up, hat, *parts],
        scratch=[
            ((seq_len, 3 * width), low),
            ((seq_len, width), wide),
            ((seq_len, width), wide),
            ((seq_len, width), low),
            ((3, seq_len, width), wide),
            ((seq_len, units), low),
            ((depth, seq_len), low),
            ((depth, 3 * width + units), low),
            ((seq_len, 3 * width), low),
            ((seq_len, width), wide),
            ((seq_len, width), wide),
            ((members, half, depth), wide),
            ((members, half, depth), low),
            ((members, half, 3 * width), low),
            ((members, half, 3 * width), low),
            ((members, half, units), low),
            ((members, half, units), low),
            ((depth, 3 * width), low),
            ((quarters, 16, 3 * width), low),
        ],
        copies=7 + quarters + 2 + 2 * quarters,
        after=[branches],
        flops=1,
        memory=60,
    )
    late = messages[:1] + [send(messages[step], "fsdp", step) for step in range(1, quarters)]

    for piece in branch_pieces:
        branches = branches + piece.astype(wide)
    *early, sums = call(
        lambda *refs: share_early_kernel(members, quarters, *refs),
        [((lines + 16, width + 2 * units), low)] * members + [((1, width + 2 * units), wide)],
        place,
        *early,
        after=branch_pieces[:2],
        flops=20 * 10**9,
    )
    stay, leave = first_halving(place, kept, other, after=[sums])
    leave = send(leave, "context", 1)
    pieces = call(
        lambda *refs: share_late_kernel(members, quarters, *refs),
        [((lines + 16, 4 * width + 2 * units), low)] * members,
        place,
        *late,
        *early,
        after=[stay],
        flops=3 * 10**9,
    )
    pieces = [pieces[0]] + [send(pieces[step], "context", step) for step in others]

    own = take(tokens, core * half, half).astype(wide)
    result = both_halves((own + branches + b_out + b_down).astype(low))
    grad_norm = last_halvings(stay + leave.astype(wide))
    center = own - jnp.mean(own, axis=-1, keepdims=True)
    factor = lax.rsqrt(jnp.mean(center * center, axis=-1, keepdims=True) + EPSILON)
    normed = center * factor
    grad_input = factor * (
        grad_norm
        - jnp.mean(grad_norm, axis=-1, keepdims=True)
        - normed * jnp.mean(grad_norm * normed, axis=-1, keepdims=True)
    )
    own_grad = take(cotangent, core * half, half).astype(wide)
    grad_half = own_grad + grad_input
    grad_tokens = both_halves(grad_half)

    begin = lax.axis_index("fsdp") * part + here * lines
    columns = jnp.stack([ln1_gain, ln1_bias, ln2_gain, ln2_bias])
    grad_w_qkv, bias_qkv, grad_w_out, grad_w_up, bias_up, grad_w_down, norms = call(
        lambda *refs: owner_kernel(members, *refs),
        [
            ((3, lines, members * width), wide),
            ((3, members * width), wide),
            ((lines, members * width), wide),
            ((lines, members * units), wide),
            ((1, members * units), wide),
            ((lines, members * units), wide),
            ((lines, 128), wide),
        ],
        place,
        *pieces,
        qkv_rows,
        up_rows,
        take(columns, begin, lines, 1).T,
        after=[leave, branches],
    )
    norms = norms[:, :4].T
    norms = norms + send(norms, "tensor", 1)
    columns = take(sums[0], here * lines, lines)
    return (
        result,
        grad_tokens,
        norms[0],
        norms[1],
        norms[2],
        norms[3],
        grad_w_qkv.transpose(1, 0, 2),
        bias_qkv,
        grad_w_out,
        columns,
        grad_w_up,
        bias_up[0],
        grad_w_down,
        columns,
    )


def power_of_two(number):
    return number & (number - 1) == 0


def on_device(*arrays):
    members = lax.axis_size("context")
    local_heads = arrays[6].shape[2] // HEAD
    units = arrays[10].shape[1]
    fits = (
        members > 1
        and local_heads % members == 0
        and units % members == 0
        and lax.axis_size("tensor") == 2
        and power_of_two(members)
        and power_of_two(lax.axis_size("fsdp"))
    )
    return whole_sequences(*arrays) if fits else gathered_weights(*arrays)


def solution(mesh):
    in_specs = (
        P(("fsdp", "context"), None),
        P(("fsdp", "context"), None),
        P(),
        P(),
        P(),
        P(),
        P("fsdp", None, "tensor"),
        P(None, "tensor"),
        P("fsdp", "tensor"),
        P(),
        P("fsdp", "tensor"),
        P("tensor"),
        P("fsdp", "tensor"),
        P(),
    )
    out_specs = (
        P(("fsdp", "context"), None),
        P(("fsdp", "context"), None),
        P(("fsdp", "context")),
        P(("fsdp", "context")),
        P(("fsdp", "context")),
        P(("fsdp", "context")),
        P(("fsdp", "context"), None, "tensor"),
        P(None, "tensor"),
        P(("fsdp", "context"), "tensor"),
        P(("fsdp", "context")),
        P(("fsdp", "context"), "tensor"),
        P("tensor"),
        P(("fsdp", "context"), "tensor"),
        P(("fsdp", "context")),
    )
    return jax.shard_map(
        on_device, mesh=mesh, in_specs=in_specs, out_specs=out_specs, check_vma=False
    )
```
